1024 devices in a mesh: src: 32 (over y_lo, x), rec: 8 (over z), freq: 4 (over y_hi, core).
Axes of the slice: x: 8, y: 8 (y_hi: 2, y_lo: 4; y = y_hi * 4 + y_lo), z: 8, core: 2. Of those that a mesh axis runs over, the one named last changes fastest.
Arguments:
- wave: bfloat16 [2, 8, 2048, 4096], P(None, 'freq', 'src', 'rec'), may hold values from -6 to 6
- tap_table: float32 [2, 64, 8, 33], P(None, None, 'freq'), may hold values from -0.75 to 0.75
- src_index: int32 [3, 2048], P(None, 'src'), may hold values from 0 to 63
- rec_index: int32 [3, 4096], P(None, 'rec'), may hold values from 0 to 63
- offset_bin: int32 [2048, 4096], P('src', 'rec'), may hold values from 0 to 63
- bin_weight: float32 [3, 64], replicated, may hold values from 0.5 to 2
Outputs:
- final_wave: bfloat16 [2, 8, 2048, 4096], P(None, 'freq', 'src', 'rec')
- image: float32 [2048, 4096], P(('src', 'freq'), 'rec')
The draws below stay inside these ranges and needn't reach their ends.
All inputs are finite; a program needn't handle non-finite values.
Results may differ from the reference program's by a relative error of at most 0.012.
Values may be sent and summed in bfloat16 or wider, within the bound.
A program may use at most 32 MiB of HBM per device.

```python
import math
import jax
import jax.numpy as jnp
from jax import lax

S_DEV = 64
R_DEV = 512
F_DEV = 2
TAPS = 33
NTAB = 64
NBIN = 64
DEPTHS = 3
NS = 2048
NR = 4096
NF = 8
N_FREQ = 4


def place_ends(drawn, rng, low, largest):
    place = [jax.random.randint(jax.random.fold_in(rng, axis), (), 0, length) for axis, length in enumerate(drawn.shape)]
    main_axis = drawn.shape.index(max(drawn.shape))
    beside = place[:main_axis] + [(place[main_axis] + 1) % drawn.shape[main_axis]] + place[main_axis + 1:]
    return drawn.at[tuple(place)].set(low).at[tuple(beside)].set(largest)


def steps_of(own_key, dims, shards, least, top_value):
    loudness, own = 1.0, jax.random.fold_in(own_key, 6)
    for dim, shards_of in shards:
        steps = jnp.exp(jax.random.uniform(jax.random.fold_in(own, dim), (shards_of,), jnp.float32, least / len(shards), top_value / len(shards)))
        loudness = loudness * jnp.repeat(steps, dims[dim] // shards_of).reshape([-1 if axis == dim else 1 for axis in range(len(dims))])
    return loudness


def gaussian(key, extent, spread, limit, shards=(), kind=jnp.bfloat16):
    level = steps_of(key, extent, shards, -0.22, 0.18) if shards else 1.0
    entries = jax.random.normal(key, extent, jnp.float32) * spread * level
    return jnp.minimum(jnp.maximum(entries, -limit), limit).astype(kind)


def setup_inputs(seed: int = 0) -> dict:
    streams_of = jax.random.split(jax.random.key(seed), 7)
    return {
        "wave": gaussian(streams_of[0], (2, NF, NS, NR), 1.0, 6.0, ((1, 4), (2, 32), (3, 8))),
        "tap_table": gaussian(streams_of[1], (2, NTAB, NF, TAPS), (2 * TAPS) ** -0.5, 0.75, ((2, 4),), jnp.float32),
        "src_index": place_ends(jax.random.randint(streams_of[2], (DEPTHS, NS), 0, NTAB), jax.random.fold_in(streams_of[2], 1), 0, NTAB - 1).astype(jnp.int32),
        "rec_index": place_ends(jax.random.randint(streams_of[3], (DEPTHS, NR), 0, NTAB), jax.random.fold_in(streams_of[3], 1), 0, NTAB - 1).astype(jnp.int32),
        "offset_bin": place_ends(jax.random.randint(streams_of[4], (NS, NR), 0, NBIN), jax.random.fold_in(streams_of[4], 1), 0, NBIN - 1).astype(jnp.int32),
        "bin_weight": jnp.clip(jnp.exp(jax.random.uniform(streams_of[5], (DEPTHS, NBIN), jnp.float32, math.log(0.5), math.log(2.0))), 0.5, 2.0),
    }


def banded(tap_rows, block_size):
    leading = tap_rows.shape[:-2]
    tap_count = tap_rows.shape[-1]
    block_count = tap_rows.shape[-2] // block_size
    grouped = tap_rows.reshape(leading + (block_count, block_size, tap_count))
    padded = jnp.pad(grouped, [(0, 0)] * (len(leading) + 2) + [(0, block_size)])
    flattened = padded.reshape(leading + (block_count, block_size * (tap_count + block_size)))
    flattened = flattened[..., :block_size * (block_size + tap_count - 1)]
    return flattened.reshape(leading + (block_count, block_size, block_size + tap_count - 1))

def operator_pair(tap_rows, block_size):
    matrices = banded(tap_rows, block_size)
    real_part = jnp.concatenate([matrices[0], -matrices[1]], axis=-1)
    imag_part = jnp.concatenate([matrices[1], matrices[0]], axis=-1)
    return (real_part, imag_part)

def receiver_pass(padded, operators, block_size):
    block_count = operators[0].shape[1]
    extra = (block_count + 1) * block_size - padded.shape[3]
    widened = jnp.pad(padded, ((0, 0), (0, 0), (0, 0), (0, extra)))
    grouped = widened.reshape(padded.shape[:3] + (block_count + 1, block_size))
    windows = jnp.concatenate([grouped[..., :block_count, :], grouped[..., 1:, :TAPS - 1]], axis=-1)
    stacked = jnp.concatenate([windows[0], windows[1]], axis=-1).astype(jnp.float32)
    real_out = jnp.einsum('fsnj,fncj->fsnc', stacked, operators[0].astype(jnp.float32), precision=lax.Precision.HIGHEST)
    imag_out = jnp.einsum('fsnj,fncj->fsnc', stacked, operators[1].astype(jnp.float32), precision=lax.Precision.HIGHEST)
    result = jnp.stack([real_out, imag_out]).reshape(padded.shape[:3] + (block_count * block_size,))
    return result.astype(jnp.bfloat16)

def source_pass(padded, operators, block_size):
    block_count = operators[0].shape[1]
    extra = (block_count + 1) * block_size - padded.shape[2]
    widened = jnp.pad(padded, ((0, 0), (0, 0), (0, extra), (0, 0)))
    grouped = widened.reshape(padded.shape[:2] + (block_count + 1, block_size, padded.shape[3]))
    windows = jnp.concatenate([grouped[:, :, :block_count], grouped[:, :, 1:, :TAPS - 1]], axis=3)
    stacked = jnp.concatenate([windows[0], windows[1]], axis=2).astype(jnp.float32)
    real_out = jnp.einsum('fnjr,fncj->fncr', stacked, operators[0].astype(jnp.float32), precision=lax.Precision.HIGHEST)
    imag_out = jnp.einsum('fnjr,fncj->fncr', stacked, operators[1].astype(jnp.float32), precision=lax.Precision.HIGHEST)
    result = jnp.stack([real_out, imag_out]).reshape(padded.shape[:2] + (block_count * block_size, padded.shape[3]))
    return result.astype(jnp.bfloat16)

def reference(wave, tap_table, src_index, rec_index, offset_bin, bin_weight):
    half_taps = TAPS // 2
    block_rec = min(128, R_DEV)
    block_src = min(128, S_DEV)
    table_bf = tap_table.astype(jnp.bfloat16)
    pair_weight = bin_weight[:, offset_bin]

    def one_frequency(inputs):
        wavefield, table_one = inputs
        image_part = jnp.zeros((NS, NR), jnp.float32)
        for depth_step in range(DEPTHS):
            rec_taps = jnp.moveaxis(table_one[:, rec_index[depth_step]], 1, 2)
            src_taps = jnp.moveaxis(table_one[:, src_index[depth_step]], 1, 2)
            padded = jnp.pad(wavefield, ((0, 0), (0, 0), (0, 0), (half_taps, half_taps)))
            swept = receiver_pass(padded, operator_pair(rec_taps, block_rec), block_rec)
            padded = jnp.pad(swept, ((0, 0), (0, 0), (half_taps, half_taps), (0, 0)))
            wavefield = source_pass(padded, operator_pair(src_taps, block_src), block_src)
            image_part = image_part + pair_weight[depth_step] * wavefield[0, 0].astype(jnp.float32)
        return (wavefield, image_part)
    per_wave = jnp.moveaxis(wave, 1, 0)[:, :, None]
    per_table = jnp.moveaxis(table_bf, 2, 0)[:, :, :, None]
    waves_out, images = lax.map(one_frequency, (per_wave, per_table))
    partial_value = lax.optimization_barrier(jnp.sum(images.reshape((N_FREQ, F_DEV, NS, NR)), axis=1)).astype(jnp.bfloat16)
    total = lax.optimization_barrier(jnp.sum(partial_value.astype(jnp.float32), axis=0))
    image = total * (1.0 / math.sqrt(NF * DEPTHS))
    final_wave = jnp.moveaxis(waves_out[:, :, 0], 0, 1)
    return (final_wave, image)
```

```python
import functools
import math

import jax
import jax.numpy as jnp
from jax import lax
from jax.experimental import pallas as pl
from jax.experimental.pallas import tpu as pltpu
from jax.sharding import PartitionSpec as P

MESH = pl.DeviceIdType.MESH
TAPS = 33
HALF = TAPS // 2
DEPTHS = 3
HALO = HALF * DEPTHS
LANE = 128
PAD = LANE
BF = jnp.bfloat16
F32 = jnp.float32


def across(a, b):
    return lax.dot_general(a, b, (((1,), (1,)), ((), ())), preferred_element_type=F32)


def columns_of(rows):
    n = rows.shape[1]
    eye = lax.broadcasted_iota(jnp.int32, (n, n), 0) == lax.broadcasted_iota(jnp.int32, (n, n), 1)
    return across(eye.astype(BF), rows.astype(F32).astype(BF))


def onehot_of(column, entries):
    places = lax.broadcasted_iota(jnp.int32, (column.shape[0], entries), 1).astype(F32)
    return jnp.where(column == places, 1.0, 0.0).astype(BF)


def band(taps, base):
    m = taps.shape[0]
    turned = pltpu.roll(taps, base, 1, stride=1, stride_axis=0)
    lane = lax.broadcasted_iota(jnp.int32, (m, LANE), 1)
    row = lax.broadcasted_iota(jnp.int32, (m, LANE), 0)
    place = lane - row - base
    first = jnp.where(place >= 0, turned, 0.0)
    second = jnp.where((place < 0) & (place >= -LANE), turned, 0.0)
    return first.astype(BF), second.astype(BF)


def kernel(
    sizes,
    wave,
    table,
    src_index,
    rec_index,
    offset_bin,
    bin_weight,
    wave_out,
    image_out,
    x0,
    x1,
    x2,
    q,
    fin,
    src_low,
    src_high,
    rec_low,
    rec_high,
    src_col,
    rec_col,
    taps_table,
    rec_taps,
    rec_op,
    src_op0,
    src_op1,
    src_op2,
    weights,
    part,
    part_bf,
    parts_in,
    own_sem,
    out_sem,
    send_sem,
    recv_sem,
    index_send,
    index_recv,
    part_send,
    part_recv,
):
    n_src, n_rec, n_freq, scale = sizes
    _, n_f, rows, cols = wave.shape
    entries = table.shape[1]
    tiles = cols // LANE
    i, j, g = lax.axis_index("src"), lax.axis_index("rec"), lax.axis_index("freq")
    has = {-1: (i > 0, j > 0), 0: (None, None), 1: (i < n_src - 1, j < n_rec - 1)}
    ways = [(0, -1), (0, 1), (-1, 0), (1, 0), (-1, -1), (-1, 1), (1, -1), (1, 1)]

    def exists(way):
        conds = [c for c in (has[way[0]][0], has[way[1]][1]) if c is not None]
        return functools.reduce(jnp.logical_and, conds)

    def target(way):
        where = {}
        if way[0]:
            where["src"] = i + way[0]
        if way[1]:
            where["rec"] = j + way[1]
        return where

    for f in range(n_f):
        for c in range(2):
            x0[f, c, :HALO, :] = jnp.zeros((HALO, cols + 2 * PAD), BF)
            x0[f, c, HALO + rows :, :] = jnp.zeros((HALO, cols + 2 * PAD), BF)
            x0[f, c, HALO : HALO + rows, :PAD] = jnp.zeros((rows, PAD), BF)
            x0[f, c, HALO : HALO + rows, PAD + cols :] = jnp.zeros((rows, PAD), BF)
    for ref in (src_low, src_high, rec_low, rec_high):
        ref[...] = jnp.full(ref.shape, -1, jnp.int32)

    barrier = pltpu.get_barrier_semaphore()
    for way in ways:

        @pl.when(exists(way))
        def _(way=way):
            pl.semaphore_signal(barrier, inc=1, device_id=target(way), device_id_type=MESH)

    for d in range(1, n_freq):
        pl.semaphore_signal(
            barrier, inc=1, device_id={"freq": lax.rem(g + d, n_freq)}, device_id_type=MESH
        )
    along_src = (i > 0).astype(jnp.int32) + (i < n_src - 1).astype(jnp.int32)
    along_rec = (j > 0).astype(jnp.int32) + (j < n_rec - 1).astype(jnp.int32)

    own = [
        pltpu.make_async_copy(
            wave.at[:, f],
            x0.at[f, :, pl.ds(HALO, rows), pl.ds(PAD, cols)],
            own_sem.at[f],
        )
        for f in range(n_f)
    ]
    for copy in own:
        copy.start()
    pl.semaphore_wait(barrier, (along_src + 1) * (along_rec + 1) - 1 + n_freq - 1)

    def halo_copy(f, number, way):
        ds, dr = way
        if ds == 0:
            from_rows, to_rows = pl.ds(0, rows), pl.ds(HALO, rows)
        elif ds < 0:
            from_rows, to_rows = pl.ds(0, HALO), pl.ds(HALO + rows, HALO)
        else:
            from_rows, to_rows = pl.ds(rows - HALO, HALO), pl.ds(0, HALO)
        if dr == 0:
            from_cols, to_cols = pl.ds(0, cols), pl.ds(PAD, cols)
        elif dr < 0:
            from_cols, to_cols = pl.ds(0, PAD), pl.ds(PAD + cols, PAD)
        else:
            from_cols, to_cols = pl.ds(cols - PAD, PAD), pl.ds(0, PAD)
        return pltpu.make_async_remote_copy(
            src_ref=wave.at[:, f, from_rows, from_cols],
            dst_ref=x0.at[f, :, to_rows, to_cols],
            send_sem=send_sem.at[f, number],
            recv_sem=recv_sem.at[f, number],
            device_id=target(way),
            device_id_type=MESH,
        )

    def index_copy(number, way):
        if way[0]:
            source, dest = src_index, (src_high if way[0] < 0 else src_low)
        elif way[1] < 0:
            source, dest = rec_index.at[:, pl.ds(0, PAD)], rec_high
        else:
            source, dest = rec_index.at[:, pl.ds(cols - PAD, PAD)], rec_low
        return pltpu.make_async_remote_copy(
            src_ref=source,
            dst_ref=dest,
            send_sem=index_send.at[number],
            recv_sem=index_recv.at[number],
            device_id=target(way),
            device_id_type=MESH,
        )

    for number, way in enumerate(ways[:4]):

        @pl.when(exists(way))
        def _(number=number, way=way):
            index_copy(number, way).start()

    for f in range(n_f):
        for number, way in enumerate(ways):

            @pl.when(exists(way))
            def _(f=f, number=number, way=way):
                halo_copy(f, number, way).start()

    taps_table[...] = jnp.zeros(taps_table.shape, BF)
    for f in range(n_f):
        for c in range(2):
            first = (2 * f + c) * LANE
            taps_table[:, first : first + TAPS] = table[c, :, f, :].astype(BF)

    for t in range(tiles):
        at = slice(t * LANE, (t + 1) * LANE)
        bins = offset_bin[:, at]
        for z in range(DEPTHS):
            line = jnp.concatenate(
                [bin_weight[z : z + 1, :], jnp.zeros((1, LANE - bin_weight.shape[1]), F32)], axis=1
            )
            spread = jnp.broadcast_to(line, (rows, LANE))
            weights[z, :, at] = jnp.take_along_axis(
                spread, bins, axis=1, mode="promise_in_bounds"
            )

    for number, way in enumerate(ways[:4]):

        @pl.when(exists(way))
        def _(number=number, way=way):
            index_copy(number, way).wait_send()

        @pl.when(exists((-way[0], -way[1])))
        def _(number=number, way=way):
            index_copy(number, way).wait_recv()

    src_col[:rows, :] = columns_of(src_low[...])
    src_col[rows : 2 * rows, :] = columns_of(src_index[...])
    src_col[2 * rows :, :] = columns_of(src_high[...])
    rec_col[:PAD, :] = columns_of(rec_low[...])
    for t in range(tiles):
        rec_col[PAD + t * LANE : PAD + (t + 1) * LANE, :] = columns_of(
            rec_index[:, t * LANE : (t + 1) * LANE]
        )
    rec_col[PAD + cols :, :] = columns_of(rec_high[...])

    for z, op in enumerate((src_op0, src_op1, src_op2)):
        left = HALO - HALF * (z + 1)
        n_out = rows + 2 * left
        hot = onehot_of(src_col[rows - left : rows - left + n_out, z : z + 1], entries)
        taps = jnp.dot(hot, taps_table[...], preferred_element_type=F32)
        for f in range(n_f):
            for c in range(2):
                first, second = band(taps[:, (2 * f + c) * LANE : (2 * f + c + 1) * LANE], 0)
                op[f, c * n_out : (c + 1) * n_out, :LANE] = first
                if op.shape[2] > LANE:
                    op[f, c * n_out : (c + 1) * n_out, LANE:] = second

    counts = [tiles + 1, tiles + 1, tiles]
    starts = [0, counts[0], counts[0] + counts[1]]
    for z in range(DEPTHS):
        left = HALO - HALF * (z + 1)
        base = PAD - left - HALF if z == 0 else 0

        def build(n, carry, z=z, left=left, base=base):
            at = pl.multiple_of(n * LANE + (PAD - left), HALF)
            hot = onehot_of(rec_col[pl.ds(at, LANE), :][:, z : z + 1], entries)
            rec_taps[...] = jnp.dot(hot, taps_table[...], preferred_element_type=F32)
            for f in range(n_f):
                for c in range(2):
                    first, second = band(rec_taps[:, (2 * f + c) * LANE : (2 * f + c + 1) * LANE], base)
                    rec_op[f, starts[z] + n, c * LANE : (c + 1) * LANE, :LANE] = first
                    rec_op[f, starts[z] + n, c * LANE : (c + 1) * LANE, LANE:] = second
            return carry

        lax.fori_loop(0, counts[z], build, 0)

    for f in range(n_f):
        own[f].wait()
        for number, way in enumerate(ways):

            @pl.when(exists((-way[0], -way[1])))
            def _(f=f, number=number, way=way):
                halo_copy(f, number, way).wait_recv()

        held = (x0.at[f], x1, x2)
        for z in range(DEPTHS):
            left = HALO - HALF * (z + 1)
            n_in, n_out = rows + 2 * left + 2 * HALF, rows + 2 * left
            source = held[z]
            for n in range(counts[z]):
                wide = 2 * LANE if (n + 2) * LANE <= source.shape[-1] else LANE
                window = source[:, :, n * LANE : n * LANE + wide].reshape(2 * n_in, wide)
                y = across(window, rec_op[f, starts[z] + n, :, :wide])
                at = slice(n * LANE, (n + 1) * LANE)
                q[0, :n_in, at] = (y[:n_in, :LANE] - y[n_in:, LANE:]).astype(BF)
                q[1, :n_in, at] = (y[:n_in, LANE:] + y[n_in:, :LANE]).astype(BF)
            op = (src_op0, src_op1, src_op2)[z][f, :, :n_in]
            reals = []
            for n in range(counts[z]):
                at = slice(n * LANE, (n + 1) * LANE)
                pair = jnp.concatenate([q[0, :n_in, at], q[1, :n_in, at]], axis=1)
                y = jnp.dot(op, pair, preferred_element_type=F32)
                real = (y[:n_out, :LANE] - y[n_out:, LANE:]).astype(BF)
                imag = (y[:n_out, LANE:] + y[n_out:, :LANE]).astype(BF)
                if z + 1 < DEPTHS:
                    held[z + 1][0, :, at] = real
                    held[z + 1][1, :, at] = imag
                else:
                    fin[0, f, :, at] = real
                    fin[1, f, :, at] = imag
                reals.append(real[left : left + rows, :].astype(F32))
            whole = jnp.concatenate(reals, axis=1) if left else None
            if left:
                whole = pltpu.roll(whole, whole.shape[1] - left, 1)
            for t in range(tiles):
                at = slice(t * LANE, (t + 1) * LANE)
                term = weights[z, :, at] * (whole[:, at] if left else reals[t])
                if z == 0 and f == 0:
                    part[:, at] = term
                else:
                    part[:, at] = part[:, at] + term
        if f == n_f - 1:
            part_bf[...] = part[...].astype(BF)
            piece = rows // n_freq
            sends = []
            for d in range(1, n_freq):
                to = lax.rem(g + d, n_freq)
                copy = pltpu.make_async_remote_copy(
                    src_ref=part_bf.at[pl.ds(pl.multiple_of(to * piece, piece), piece)],
                    dst_ref=parts_in.at[d - 1],
                    send_sem=part_send.at[d - 1],
                    recv_sem=part_recv.at[d - 1],
                    device_id={"freq": to},
                    device_id_type=MESH,
                )
                copy.start()
                sends.append(copy)
        pltpu.make_async_copy(fin.at[:, f], wave_out.at[:, f], out_sem.at[f]).start()

    piece = rows // n_freq
    total = part_bf[pl.ds(pl.multiple_of(g * piece, piece), piece), :].astype(F32)
    for d, copy in enumerate(sends):
        copy.wait()
        total = total + parts_in[d].astype(F32)
    image_out[...] = total * scale

    for f in range(n_f):
        pltpu.make_async_copy(fin.at[:, f], wave_out.at[:, f], out_sem.at[f]).wait()
        for number, way in enumerate(ways):

            @pl.when(exists(way))
            def _(f=f, number=number, way=way):
                halo_copy(f, number, way).wait_send()


def shards(wave, tap_table, src_index, rec_index, offset_bin, bin_weight):
    n_src, n_rec, n_freq = (lax.axis_size(a) for a in ("src", "rec", "freq"))
    _, n_f, rows, cols = wave.shape
    scale = 1.0 / math.sqrt(n_f * n_freq * DEPTHS)
    tiles = cols // LANE
    piece = rows // n_freq
    outs = [rows + 2 * (HALO - HALF * (z + 1)) for z in range(DEPTHS)]
    vmem = pl.BlockSpec(memory_space=pltpu.VMEM)
    anywhere = pl.BlockSpec(memory_space=pl.ANY)
    dma = pltpu.SemaphoreType.DMA
    return pl.pallas_call(
        functools.partial(kernel, (n_src, n_rec, n_freq, scale)),
        out_shape=(
            jax.ShapeDtypeStruct(wave.shape, BF),
            jax.ShapeDtypeStruct((piece, cols), F32),
        ),
        in_specs=[anywhere, vmem, vmem, vmem, vmem, vmem],
        out_specs=(anywhere, vmem),
        scratch_shapes=[
            pltpu.VMEM((n_f, 2, rows + 2 * HALO, cols + 2 * PAD), BF),
            pltpu.VMEM((2, outs[0], cols + LANE), BF),
            pltpu.VMEM((2, outs[1], cols + LANE), BF),
            pltpu.VMEM((2, rows + 2 * HALO, cols + LANE), BF),
            pltpu.VMEM((2, n_f, rows, cols), BF),
            pltpu.VMEM((DEPTHS, rows), jnp.int32),
            pltpu.VMEM((DEPTHS, rows), jnp.int32),
            pltpu.VMEM((DEPTHS, PAD), jnp.int32),
            pltpu.VMEM((DEPTHS, PAD), jnp.int32),
            pltpu.VMEM((3 * rows, DEPTHS), F32),
            pltpu.VMEM((cols + 2 * PAD, DEPTHS), F32),
            pltpu.VMEM((tap_table.shape[1], n_f * 2 * LANE), BF),
            pltpu.VMEM((LANE, n_f * 2 * LANE), F32),
            pltpu.VMEM((n_f, 3 * tiles + 2, 2 * LANE, 2 * LANE), BF),
            pltpu.VMEM((n_f, 2 * outs[0], 2 * LANE), BF),
            pltpu.VMEM((n_f, 2 * outs[1], LANE), BF),
            pltpu.VMEM((n_f, 2 * outs[2], LANE), BF),
            pltpu.VMEM((DEPTHS, rows, cols), F32),
            pltpu.VMEM((rows, cols), F32),
            pltpu.VMEM((rows, cols), BF),
            pltpu.VMEM((max(n_freq - 1, 1), piece, cols), BF),
            dma((n_f,)),
            dma((n_f,)),
            dma((n_f, 8)),
            dma((n_f, 8)),
            dma((4,)),
            dma((4,)),
            dma((max(n_freq - 1, 1),)),
            dma((max(n_freq - 1, 1),)),
        ],
        compiler_params=pltpu.CompilerParams(
            collective_id=0, has_side_effects=True, vmem_limit_bytes=32 * 1024 * 1024
        ),
    )(wave, tap_table, src_index, rec_index, offset_bin, bin_weight)


def solution(mesh):
    placed = (
        P(None, "freq", "src", "rec"),
        P(None, None, "freq", None),
        P(None, "src"),
        P(None, "rec"),
        P("src", "rec"),
        P(),
    )
    return jax.shard_map(
        shards,
        mesh=mesh,
        in_specs=placed,
        out_specs=(P(None, "freq", "src", "rec"), P(("src", "freq"), "rec")),
        check_vma=False,
    )
```

```python
import functools
import math

import jax
import jax.numpy as jnp
from jax import lax
from jax.experimental import pallas as pl
from jax.experimental.pallas import tpu as pltpu
from jax.sharding import PartitionSpec as P

MESH = pl.DeviceIdType.MESH
TAPS = 33
HALF = TAPS // 2
DEPTHS = 3
HALO = HALF * DEPTHS
LANE = 128
PAD = LANE
BF = jnp.bfloat16
F32 = jnp.float32


def across(a, b):
    return lax.dot_general(a, b, (((1,), (1,)), ((), ())), preferred_element_type=F32)


def columns_of(rows):
    n = rows.shape[1]
    eye = lax.broadcasted_iota(jnp.int32, (n, n), 0) == lax.broadcasted_iota(jnp.int32, (n, n), 1)
    return across(eye.astype(BF), rows.astype(F32).astype(BF))


def onehot_of(column, entries):
    places = lax.broadcasted_iota(jnp.int32, (column.shape[0], entries), 1).astype(F32)
    return jnp.where(column == places, 1.0, 0.0).astype(BF)


def band(taps, base):
    m = taps.shape[0]
    turned = pltpu.roll(taps, base, 1, stride=1, stride_axis=0)
    lane = lax.broadcasted_iota(jnp.int32, (m, LANE), 1)
    row = lax.broadcasted_iota(jnp.int32, (m, LANE), 0)
    place = lane - row - base
    first = jnp.where(place >= 0, turned, 0.0)
    second = jnp.where((place < 0) & (place >= -LANE), turned, 0.0)
    return first.astype(BF), second.astype(BF)


def kernel(
    sizes,
    wave,
    table_in,
    src_index_in,
    rec_index_in,
    offset_bin_in,
    bin_weight_in,
    fin,
    part_own,
    parts_in,
    table,
    src_index,
    rec_index,
    offset_bin,
    bin_weight,
    in_sem,
    x0,
    x1,
    x2,
    q,
    src_low,
    src_high,
    rec_low,
    rec_high,
    src_col,
    rec_col,
    taps_table,
    rec_taps,
    rec_op,
    src_op0,
    src_op1,
    src_op2,
    weights,
    part,
    part_bf,
    own_sem,
    send_sem,
    recv_sem,
    index_send,
    index_recv,
    part_send,
    part_recv,
    ready,
    peer_ready,
):
    n_src, n_rec, n_freq = sizes
    _, n_f, rows, cols = wave.shape
    entries = table.shape[3]
    tiles = cols // LANE
    i, j, g = lax.axis_index("src"), lax.axis_index("rec"), lax.axis_index("freq")
    has = {-1: (i > 0, j > 0), 0: (None, None), 1: (i < n_src - 1, j < n_rec - 1)}
    ways = [(-1, 0), (1, 0), (0, -1), (0, 1), (-1, -1), (-1, 1), (1, -1), (1, 1)]

    def exists(way):
        conds = [c for c in (has[way[0]][0], has[way[1]][1]) if c is not None]
        return functools.reduce(jnp.logical_and, conds)

    def target(way):
        where = {}
        if way[0]:
            where["src"] = i + way[0]
        if way[1]:
            where["rec"] = j + way[1]
        return where

    barrier = pltpu.get_barrier_semaphore()
    for way in ways:
        if way[1] >= 0:

            @pl.when(exists(way))
            def _(way=way):
                pl.semaphore_signal(barrier, inc=1, device_id=target(way), device_id_type=MESH)

    for d in range(1, n_freq):

        @pl.when(g >= d)
        def _(d=d):
            pl.semaphore_signal(barrier, inc=1, device_id={"freq": g - d}, device_id_type=MESH)

    fetch = [
        pltpu.make_async_copy(source, dest, in_sem.at[k])
        for k, (source, dest) in enumerate(
            [
                (src_index_in, src_index),
                (rec_index_in, rec_index),
                (table_in, table),
                (bin_weight_in, bin_weight),
                (offset_bin_in, offset_bin),
            ]
        )
    ]
    for copy in fetch:
        copy.start()
    own = [
        pltpu.make_async_copy(
            wave.at[:, f],
            x0.at[f, :, pl.ds(HALO, rows), pl.ds(PAD, cols)],
            own_sem.at[f],
        )
        for f in range(n_f)
    ]
    for copy in own:
        copy.start()

    along_src = (i > 0).astype(jnp.int32) + (i < n_src - 1).astype(jnp.int32)
    below_rec = (j > 0).astype(jnp.int32)

    def halo_copy(f, number, way):
        ds, dr = way
        from_rows = [pl.ds(0, rows), pl.ds(rows - HALO, HALO), pl.ds(0, HALO)][ds]
        to_rows = [pl.ds(HALO, rows), pl.ds(0, HALO), pl.ds(HALO + rows, HALO)][ds]
        from_cols = [pl.ds(0, cols), pl.ds(cols - PAD, PAD), pl.ds(0, PAD)][dr]
        to_cols = [pl.ds(PAD, cols), pl.ds(0, PAD), pl.ds(PAD + cols, PAD)][dr]
        return pltpu.make_async_remote_copy(
            src_ref=wave.at[:, f, from_rows, from_cols],
            dst_ref=x0.at[f, :, to_rows, to_cols],
            send_sem=send_sem.at[f, number],
            recv_sem=recv_sem.at[f, number],
            device_id=target(way),
            device_id_type=MESH,
        )

    def index_copy(number, way):
        if way[0]:
            source, dest = src_index_in, (src_high if way[0] < 0 else src_low)
        elif way[1] < 0:
            source, dest = rec_index_in.at[:, pl.ds(0, PAD)], rec_high
        else:
            source, dest = rec_index_in.at[:, pl.ds(cols - PAD, PAD)], rec_low
        return pltpu.make_async_remote_copy(
            src_ref=source,
            dst_ref=dest,
            send_sem=index_send.at[number],
            recv_sem=index_recv.at[number],
            device_id=target(way),
            device_id_type=MESH,
        )

    counts = [tiles + 1, tiles + 1, tiles]
    starts = [0, counts[0], counts[0] + counts[1]]
    lefts = [HALO - HALF * (z + 1) for z in range(DEPTHS)]

    def build_rec(z, blocks):
        base = PAD - lefts[z] - HALF if z == 0 else 0
        for n in blocks:
            at = n * LANE + PAD - lefts[z]
            hot = onehot_of(rec_col[at : at + LANE, z : z + 1], entries)
            slot = starts[z] + n
            rec_taps[slot] = across(hot, taps_table[...])
        for n in blocks:
            slot = starts[z] + n
            for f in range(n_f):
                for c in range(2):
                    first = (2 * f + c) * LANE
                    low, high = band(rec_taps[slot, :, first : first + LANE], base)
                    rec_op[f, slot, c * LANE : (c + 1) * LANE, :LANE] = low
                    rec_op[f, slot, c * LANE : (c + 1) * LANE, LANE:] = high

    def build_src(z):
        op = (src_op0, src_op1, src_op2)[z]
        n_out = rows + 2 * lefts[z]
        hot = onehot_of(src_col[rows - lefts[z] : rows - lefts[z] + n_out, z : z + 1], entries)
        taps = across(hot, taps_table[...])
        for f in range(n_f):
            for c in range(2):
                low, high = band(taps[:, (2 * f + c) * LANE : (2 * f + c + 1) * LANE], 0)
                op[f, c * n_out : (c + 1) * n_out, :LANE] = low
                if op.shape[2] > LANE:
                    op[f, c * n_out : (c + 1) * n_out, LANE:] = high

    for way in ways:

        @pl.when(jnp.logical_not(exists(way)))
        def _(way=way):
            ds, dr = way
            at_rows = [slice(HALO, HALO + rows), slice(HALO + rows, None), slice(0, HALO)][ds]
            at_cols = [slice(PAD, PAD + cols), slice(PAD + cols, None), slice(0, PAD)][dr]
            for f in range(n_f):
                for c in range(2):
                    shape = x0[f, c, at_rows, at_cols].shape
                    x0[f, c, at_rows, at_cols] = jnp.zeros(shape, BF)
            if ds == 0 or dr == 0:
                ref = ((rec_high, rec_low) if ds == 0 else (src_high, src_low))[ds + dr < 0]
                ref[...] = jnp.full(ref.shape, -1, jnp.int32)

    taps_table[...] = jnp.zeros(taps_table.shape, BF)
    for copy in fetch:
        copy.wait()
    for f in range(n_f):
        for c in range(2):
            first = (2 * f + c) * LANE
            taps_table[first : first + TAPS, :] = table[c, :, f, :].astype(BF)

    src_col[rows : 2 * rows, :] = columns_of(src_index[...])
    for t in range(tiles):
        rec_col[PAD + t * LANE : PAD + (t + 1) * LANE, :] = columns_of(
            rec_index[:, t * LANE : (t + 1) * LANE]
        )
    for z in range(DEPTHS):
        build_rec(z, range(counts[z]) if lefts[z] == 0 else range(1, counts[z] - 1))

    pl.semaphore_wait(barrier, along_src + (along_src + 1) * below_rec + n_freq - 1 - g)
    for number, way in enumerate(ways):
        if way[1] < 0:

            @pl.when(exists(way))
            def _(number=number, way=way):
                pl.semaphore_signal(
                    ready.at[number], inc=1, device_id=target(way), device_id_type=MESH
                )

    for d in range(1, n_freq):

        @pl.when(g + d < n_freq)
        def _(d=d):
            pl.semaphore_signal(
                peer_ready.at[d - 1], inc=1, device_id={"freq": g + d}, device_id_type=MESH
            )

    def send(f, number, way):
        if f == 0 and number < 4:
            index_copy(number, way).start()
        halo_copy(f, number, way).start()

    for f in range(n_f):
        for number, way in enumerate(ways):
            if way[1] <= 0:

                @pl.when(exists(way))
                def _(f=f, number=number, way=way):
                    send(f, number, way)


    for t in range(tiles):
        at = slice(t * LANE, (t + 1) * LANE)
        bins = offset_bin[:, at]
        for z in range(DEPTHS):
            line = jnp.concatenate(
                [bin_weight[z : z + 1, :], jnp.zeros((1, LANE - bin_weight.shape[1]), F32)], axis=1
            )
            spread = jnp.broadcast_to(line, (rows, LANE))
            weights[z, :, at] = jnp.take_along_axis(
                spread, bins, axis=1, mode="promise_in_bounds"
            )

    for f in range(n_f):
        for number, way in enumerate(ways):
            if way[1] > 0:

                @pl.when(exists(way))
                def _(f=f, number=number, way=way):
                    if f == 0:
                        back = ways.index((-way[0], -way[1]))
                        pl.semaphore_wait(ready.at[back], 1)
                    send(f, number, way)

    for number, way in enumerate(ways[:4]):

        @pl.when(exists((-way[0], -way[1])))
        def _(number=number, way=way):
            index_copy(number, way).wait_recv()

    src_col[:rows, :] = columns_of(src_low[...])
    src_col[2 * rows :, :] = columns_of(src_high[...])
    rec_col[:PAD, :] = columns_of(rec_low[...])
    rec_col[PAD + cols :, :] = columns_of(rec_high[...])
    for z in range(DEPTHS):
        if lefts[z]:
            build_rec(z, (0, counts[z] - 1))
        build_src(z)

    sends = []
    for f in range(n_f):
        own[f].wait()
        for number, way in enumerate(ways):

            @pl.when(exists((-way[0], -way[1])))
            def _(f=f, number=number, way=way):
                halo_copy(f, number, way).wait_recv()

        held = (x0.at[f], x1, x2)
        for z in range(DEPTHS):
            left = lefts[z]
            n_in, n_out = rows + 2 * left + 2 * HALF, rows + 2 * left
            source = held[z]
            for n in range(counts[z]):
                wide = 2 * LANE if (n + 2) * LANE <= source.shape[-1] else LANE
                window = source[:, :, n * LANE : n * LANE + wide].reshape(2 * n_in, wide)
                y = across(window, rec_op[f, starts[z] + n, :, :wide])
                at = slice(n * LANE, (n + 1) * LANE)
                q[0, :n_in, at] = (y[:n_in, :LANE] - y[n_in:, LANE:]).astype(BF)
                q[1, :n_in, at] = (y[:n_in, LANE:] + y[n_in:, :LANE]).astype(BF)
            op = (src_op0, src_op1, src_op2)[z][f, :, :n_in]
            reals = []
            for n in range(counts[z]):
                at = slice(n * LANE, (n + 1) * LANE)
                pair = jnp.concatenate([q[0, :n_in, at], q[1, :n_in, at]], axis=1)
                y = jnp.dot(op, pair, preferred_element_type=F32)
                real = (y[:n_out, :LANE] - y[n_out:, LANE:]).astype(BF)
                imag = (y[:n_out, LANE:] + y[n_out:, :LANE]).astype(BF)
                if z + 1 < DEPTHS:
                    held[z + 1][0, :, at] = real
                    held[z + 1][1, :, at] = imag
                else:
                    fin[0, f, :, at] = real
                    fin[1, f, :, at] = imag
                reals.append(real[left : left + rows, :].astype(F32))
            whole = jnp.concatenate(reals, axis=1) if left else None
            if left:
                whole = pltpu.roll(whole, whole.shape[1] - left, 1)
            for t in range(tiles):
                at = slice(t * LANE, (t + 1) * LANE)
                term = weights[z, :, at] * (whole[:, at] if left else reals[t])
                if z == 0 and f == 0:
                    part[:, at] = term
                elif z + 1 == DEPTHS and f == n_f - 1:
                    part_bf[:, at] = (part[:, at] + term).astype(BF)
                else:
                    part[:, at] = part[:, at] + term

    for d in range(1, n_freq):

        @pl.when(g >= d)
        def _(d=d):
            pl.semaphore_wait(peer_ready.at[d - 1], 1)

    piece = rows // n_freq
    for d in range(1, n_freq):
        to = lax.rem(g + d, n_freq)
        copy = pltpu.make_async_remote_copy(
            src_ref=part_bf.at[pl.ds(pl.multiple_of(to * piece, piece), piece)],
            dst_ref=parts_in.at[d - 1],
            send_sem=part_send.at[d - 1],
            recv_sem=part_recv.at[d - 1],
            device_id={"freq": to},
            device_id_type=MESH,
        )
        copy.start()
        sends.append(copy)
    part_own[...] = part_bf[pl.ds(pl.multiple_of(g * piece, piece), piece), :]
    for f in range(n_f):
        for number, way in enumerate(ways):

            @pl.when(exists(way))
            def _(f=f, number=number, way=way):
                if f == 0 and number < 4:
                    index_copy(number, way).wait_send()
                halo_copy(f, number, way).wait_send()

    for copy in sends:
        copy.wait()


def finish(scale, fin, part_own, parts_in, wave_out, image_out, image, sems):
    copies = [
        pltpu.make_async_copy(fin, wave_out, sems.at[0]),
        pltpu.make_async_copy(image, image_out, sems.at[1]),
    ]
    copies[0].start()
    total = part_own[...].astype(F32)
    for d in range(parts_in.shape[0]):
        total = total + parts_in[d].astype(F32)
    image[...] = total * scale
    copies[1].start()
    for copy in copies:
        copy.wait()


def shards(wave, tap_table, src_index, rec_index, offset_bin, bin_weight):
    n_src, n_rec, n_freq = (lax.axis_size(a) for a in ("src", "rec", "freq"))
    _, n_f, rows, cols = wave.shape
    scale = 1.0 / math.sqrt(n_f * n_freq * DEPTHS)
    tiles = cols // LANE
    piece = rows // n_freq
    outs = [rows + 2 * (HALO - HALF * (z + 1)) for z in range(DEPTHS)]
    vmem = pl.BlockSpec(memory_space=pltpu.VMEM)
    hbm = pl.BlockSpec(memory_space=pltpu.HBM)
    dma = pltpu.SemaphoreType.DMA
    operands = [
        pltpu.with_memory_space_constraint(x, pltpu.HBM)
        for x in (wave, jnp.transpose(tap_table, (0, 3, 2, 1)), src_index, rec_index, offset_bin, bin_weight)
    ]
    results = pl.pallas_call(
        functools.partial(kernel, (n_src, n_rec, n_freq)),
        out_shape=(
            pltpu.VMEM(wave.shape, BF),
            pltpu.VMEM((piece, cols), BF),
            pltpu.VMEM((n_freq - 1, piece, cols), BF),
        ),
        in_specs=[hbm] * 6,
        out_specs=(vmem, vmem, vmem),
        scratch_shapes=[
            pltpu.VMEM((2, TAPS, n_f, tap_table.shape[1]), F32),
            pltpu.VMEM(src_index.shape, jnp.int32),
            pltpu.VMEM(rec_index.shape, jnp.int32),
            pltpu.VMEM(offset_bin.shape, jnp.int32),
            pltpu.VMEM(bin_weight.shape, F32),
            dma((5,)),
            pltpu.VMEM((n_f, 2, rows + 2 * HALO, cols + 2 * PAD), BF),
            pltpu.VMEM((2, outs[0], cols + LANE), BF),
            pltpu.VMEM((2, outs[1], cols + LANE), BF),
            pltpu.VMEM((2, rows + 2 * HALO, cols + LANE), BF),
            pltpu.VMEM((DEPTHS, rows), jnp.int32),
            pltpu.VMEM((DEPTHS, rows), jnp.int32),
            pltpu.VMEM((DEPTHS, PAD), jnp.int32),
            pltpu.VMEM((DEPTHS, PAD), jnp.int32),
            pltpu.VMEM((3 * rows, DEPTHS), F32),
            pltpu.VMEM((cols + 2 * PAD, DEPTHS), F32),
            pltpu.VMEM((n_f * 2 * LANE, tap_table.shape[1]), BF),
            pltpu.VMEM((3 * tiles + 2, LANE, n_f * 2 * LANE), F32),
            pltpu.VMEM((n_f, 3 * tiles + 2, 2 * LANE, 2 * LANE), BF),
            pltpu.VMEM((n_f, 2 * outs[0], 2 * LANE), BF),
            pltpu.VMEM((n_f, 2 * outs[1], LANE), BF),
            pltpu.VMEM((n_f, 2 * outs[2], LANE), BF),
            pltpu.VMEM((DEPTHS, rows, cols), F32),
            pltpu.VMEM((rows, cols), F32),
            pltpu.VMEM((rows, cols), BF),
            dma((n_f,)),
            dma((n_f, 8)),
            dma((n_f, 8)),
            dma((4,)),
            dma((4,)),
            dma((n_freq - 1,)),
            dma((n_freq - 1,)),
            pltpu.SemaphoreType.REGULAR((8,)),
            pltpu.SemaphoreType.REGULAR((n_freq - 1,)),
        ],
        compiler_params=pltpu.CompilerParams(
            collective_id=0, has_side_effects=True, vmem_limit_bytes=40 * 1024 * 1024
        ),
    )(*operands)
    return pl.pallas_call(
        functools.partial(finish, scale),
        out_shape=(
            jax.ShapeDtypeStruct(wave.shape, BF),
            jax.ShapeDtypeStruct((piece, cols), F32),
        ),
        in_specs=[vmem] * 3,
        out_specs=(hbm, hbm),
        scratch_shapes=[pltpu.VMEM((piece, cols), F32), dma((2,))],
        compiler_params=pltpu.CompilerParams(vmem_limit_bytes=4 * 1024 * 1024),
    )(*[pltpu.with_memory_space_constraint(x, pltpu.VMEM) for x in results])


def solution(mesh):
    placed = (
        P(None, "freq", "src", "rec"),
        P(None, None, "freq", None),
        P(None, "src"),
        P(None, "rec"),
        P("src", "rec"),
        P(),
    )
    return jax.shard_map(
        shards,
        mesh=mesh,
        in_specs=placed,
        out_specs=(P(None, "freq", "src", "rec"), P(("src", "freq"), "rec")),
        check_vma=False,
    )
```

```python
import functools
import math

import jax
import jax.numpy as jnp
from jax import lax
from jax.experimental import pallas as pl
from jax.experimental.pallas import tpu as pltpu
from jax.sharding import PartitionSpec as P

MESH = pl.DeviceIdType.MESH
TAPS = 33
HALF = TAPS // 2
DEPTHS = 3
HALO = HALF * DEPTHS
LANE = 128
PAD = LANE
BF = jnp.bfloat16
F32 = jnp.float32


def across(a, b):
    return lax.dot_general(a, b, (((1,), (1,)), ((), ())), preferred_element_type=F32)


def columns_of(rows):
    n = rows.shape[1]
    eye = lax.broadcasted_iota(jnp.int32, (n, n), 0) == lax.broadcasted_iota(jnp.int32, (n, n), 1)
    return across(eye.astype(BF), rows.astype(F32).astype(BF))


def onehot_of(column, entries):
    places = lax.broadcasted_iota(jnp.int32, (column.shape[0], entries), 1).astype(F32)
    return jnp.where(column == places, 1.0, 0.0).astype(BF)


def band(taps, base):
    m = taps.shape[0]
    turned = pltpu.roll(taps, base, 1, stride=1, stride_axis=0)
    lane = lax.broadcasted_iota(jnp.int32, (m, LANE), 1)
    row = lax.broadcasted_iota(jnp.int32, (m, LANE), 0)
    place = lane - row - base
    first = jnp.where(place >= 0, turned, 0.0)
    second = jnp.where((place < 0) & (place >= -LANE), turned, 0.0)
    return first.astype(BF), second.astype(BF)


def kernel(
    sizes,
    wave,
    table_in,
    src_index_in,
    rec_index_in,
    offset_bin_in,
    bin_weight_in,
    fin,
    part_own,
    parts_in,
    table,
    src_index,
    rec_index,
    offset_bin,
    bin_weight,
    in_sem,
    x0,
    x1,
    x2,
    q,
    src_low,
    src_high,
    rec_low,
    rec_high,
    src_col,
    rec_col,
    taps_table,
    rec_taps,
    rec_op,
    src_op0,
    src_op1,
    src_op2,
    weights,
    part,
    part_bf,
    own_sem,
    send_sem,
    recv_sem,
    index_send,
    index_recv,
    part_send,
    part_recv,
    ready,
    peer_ready,
):
    n_src, n_rec, n_freq = sizes
    _, n_f, rows, cols = wave.shape
    entries = table.shape[3]
    tiles = cols // LANE
    i, j, g = lax.axis_index("src"), lax.axis_index("rec"), lax.axis_index("freq")
    has = {-1: (i > 0, j > 0), 0: (None, None), 1: (i < n_src - 1, j < n_rec - 1)}
    ways = [(-1, 0), (1, 0), (0, -1), (0, 1), (-1, -1), (-1, 1), (1, -1), (1, 1)]

    def exists(way):
        conds = [c for c in (has[way[0]][0], has[way[1]][1]) if c is not None]
        return functools.reduce(jnp.logical_and, conds)

    def target(way):
        where = {}
        if way[0]:
            where["src"] = i + way[0]
        if way[1]:
            where["rec"] = j + way[1]
        return where

    is_origin = (i == 0) & (j == 0) & (g == 0)
    rank = jnp.where((i == 0) & (j == 0), lax.rem(g + n_freq - 1, n_freq), g)

    def toward_first(way):
        return (i + way[0] == 0) & (j + way[1] == 0) & (g == 0)

    def greets(way):
        side = exists(way) & jnp.logical_not(is_origin)
        return side & toward_first(way) if way[1] < 0 else side

    def greeted(way):
        side = exists(way) & jnp.logical_not(toward_first(way))
        return side & is_origin if way[1] > 0 else side

    barrier = pltpu.get_barrier_semaphore()
    for way in ways:

        @pl.when(greets(way))
        def _(way=way):
            pl.semaphore_signal(barrier, inc=1, device_id=target(way), device_id_type=MESH)

    for d in range(1, n_freq):

        @pl.when(rank + d < n_freq)
        def _(d=d):
            pl.semaphore_signal(
                barrier, inc=1, device_id={"freq": lax.rem(g + d, n_freq)}, device_id_type=MESH
            )

    fetch = [
        pltpu.make_async_copy(source, dest, in_sem.at[k])
        for k, (source, dest) in enumerate(
            [
                (src_index_in, src_index),
                (rec_index_in, rec_index),
                (table_in, table),
                (bin_weight_in, bin_weight),
                (offset_bin_in, offset_bin),
            ]
        )
    ]
    for copy in fetch:
        copy.start()
    own = [
        pltpu.make_async_copy(
            wave.at[:, f],
            x0.at[f, :, pl.ds(HALO, rows), pl.ds(PAD, cols)],
            own_sem.at[f],
        )
        for f in range(n_f)
    ]
    for copy in own:
        copy.start()

    def halo_copy(f, number, way):
        ds, dr = way
        from_rows = [pl.ds(0, rows), pl.ds(rows - HALO, HALO), pl.ds(0, HALO)][ds]
        to_rows = [pl.ds(HALO, rows), pl.ds(0, HALO), pl.ds(HALO + rows, HALO)][ds]
        from_cols = [pl.ds(0, cols), pl.ds(cols - PAD, PAD), pl.ds(0, PAD)][dr]
        to_cols = [pl.ds(PAD, cols), pl.ds(0, PAD), pl.ds(PAD + cols, PAD)][dr]
        return pltpu.make_async_remote_copy(
            src_ref=wave.at[:, f, from_rows, from_cols],
            dst_ref=x0.at[f, :, to_rows, to_cols],
            send_sem=send_sem.at[f, number],
            recv_sem=recv_sem.at[f, number],
            device_id=target(way),
            device_id_type=MESH,
        )

    def index_copy(number, way):
        if way[0]:
            source, dest = src_index_in, (src_high if way[0] < 0 else src_low)
        elif way[1] < 0:
            source, dest = rec_index_in.at[:, pl.ds(0, PAD)], rec_high
        else:
            source, dest = rec_index_in.at[:, pl.ds(cols - PAD, PAD)], rec_low
        return pltpu.make_async_remote_copy(
            src_ref=source,
            dst_ref=dest,
            send_sem=index_send.at[number],
            recv_sem=index_recv.at[number],
            device_id=target(way),
            device_id_type=MESH,
        )

    counts = [tiles + 1, tiles + 1, tiles]
    starts = [0, counts[0], counts[0] + counts[1]]
    lefts = [HALO - HALF * (z + 1) for z in range(DEPTHS)]

    def build_rec(z, blocks):
        base = PAD - lefts[z] - HALF if z == 0 else 0
        for n in blocks:
            at = n * LANE + PAD - lefts[z]
            hot = onehot_of(rec_col[at : at + LANE, z : z + 1], entries)
            slot = starts[z] + n
            rec_taps[slot] = across(hot, taps_table[...])
        for n in blocks:
            slot = starts[z] + n
            for f in range(n_f):
                for c in range(2):
                    first = (2 * f + c) * LANE
                    low, high = band(rec_taps[slot, :, first : first + LANE], base)
                    rec_op[f, slot, c * LANE : (c + 1) * LANE, :LANE] = low
                    rec_op[f, slot, c * LANE : (c + 1) * LANE, LANE:] = high

    def build_src(z):
        op = (src_op0, src_op1, src_op2)[z]
        n_out = rows + 2 * lefts[z]
        hot = onehot_of(src_col[rows - lefts[z] : rows - lefts[z] + n_out, z : z + 1], entries)
        taps = across(hot, taps_table[...])
        for f in range(n_f):
            for c in range(2):
                low, high = band(taps[:, (2 * f + c) * LANE : (2 * f + c + 1) * LANE], 0)
                op[f, c * n_out : (c + 1) * n_out, :LANE] = low
                if op.shape[2] > LANE:
                    op[f, c * n_out : (c + 1) * n_out, LANE:] = high

    pl.semaphore_wait(barrier, sum(greeted(way).astype(jnp.int32) for way in ways) + rank)
    for number, way in enumerate(ways):

        @pl.when(greeted(way) & jnp.logical_not(greets(way)))
        def _(number=number, way=way):
            pl.semaphore_signal(
                ready.at[number], inc=1, device_id=target(way), device_id_type=MESH
            )

    for d in range(1, n_freq):

        @pl.when(rank >= d)
        def _(d=d):
            pl.semaphore_signal(
                peer_ready.at[d - 1],
                inc=1,
                device_id={"freq": lax.rem(g + n_freq - d, n_freq)},
                device_id_type=MESH,
            )

    def send(f, number, way):
        if f == 0 and number < 4:
            index_copy(number, way).start()
        halo_copy(f, number, way).start()

    for group in ((4, 6, 2), (0, 1, 3, 5, 7)):
        for f in range(n_f):
            for number in group:

                @pl.when(greeted(ways[number]))
                def _(f=f, number=number):
                    send(f, number, ways[number])

    for way in ways:

        @pl.when(jnp.logical_not(exists(way)))
        def _(way=way):
            ds, dr = way
            at_rows = [slice(HALO, HALO + rows), slice(HALO + rows, None), slice(0, HALO)][ds]
            at_cols = [slice(PAD, PAD + cols), slice(PAD + cols, None), slice(0, PAD)][dr]
            for f in range(n_f):
                for c in range(2):
                    shape = x0[f, c, at_rows, at_cols].shape
                    x0[f, c, at_rows, at_cols] = jnp.zeros(shape, BF)
            if ds == 0 or dr == 0:
                ref = ((rec_high, rec_low) if ds == 0 else (src_high, src_low))[ds + dr < 0]
                ref[...] = jnp.full(ref.shape, -1, jnp.int32)

    taps_table[...] = jnp.zeros(taps_table.shape, BF)
    for copy in fetch:
        copy.wait()
    for f in range(n_f):
        for c in range(2):
            first = (2 * f + c) * LANE
            taps_table[first : first + TAPS, :] = table[c, :, f, :].astype(BF)

    src_col[rows : 2 * rows, :] = columns_of(src_index[...])
    for t in range(tiles):
        rec_col[PAD + t * LANE : PAD + (t + 1) * LANE, :] = columns_of(
            rec_index[:, t * LANE : (t + 1) * LANE]
        )
    for z in range(DEPTHS):
        build_rec(z, range(counts[z]) if lefts[z] == 0 else range(1, counts[z] - 1))

    for t in range(tiles):
        at = slice(t * LANE, (t + 1) * LANE)
        bins = offset_bin[:, at]
        for z in range(DEPTHS):
            line = jnp.concatenate(
                [bin_weight[z : z + 1, :], jnp.zeros((1, LANE - bin_weight.shape[1]), F32)], axis=1
            )
            spread = jnp.broadcast_to(line, (rows, LANE))
            weights[z, :, at] = jnp.take_along_axis(
                spread, bins, axis=1, mode="promise_in_bounds"
            )

    for down in (False, True):
        for number, way in enumerate(ways):
            if (way[1] > 0) != down and (not down or max(way) <= 0):

                @pl.when(greets(way) & jnp.logical_not(greeted(way)))
                def _(number=number, way=way):
                    back = ways.index((-way[0], -way[1]))
                    pl.semaphore_wait(ready.at[back], 1)
                    for f in range(n_f):
                        send(f, number, way)

    for number, way in enumerate(ways[:4]):

        @pl.when(exists((-way[0], -way[1])))
        def _(number=number, way=way):
            index_copy(number, way).wait_recv()

    src_col[:rows, :] = columns_of(src_low[...])
    src_col[2 * rows :, :] = columns_of(src_high[...])
    rec_col[:PAD, :] = columns_of(rec_low[...])
    rec_col[PAD + cols :, :] = columns_of(rec_high[...])
    for z in range(DEPTHS):
        if lefts[z]:
            build_rec(z, (0, counts[z] - 1))
        build_src(z)

    sends = []
    for f in range(n_f):
        own[f].wait()
        for number, way in enumerate(ways):

            @pl.when(exists((-way[0], -way[1])))
            def _(f=f, number=number, way=way):
                halo_copy(f, number, way).wait_recv()

        held = (x0.at[f], x1, x2)
        for z in range(DEPTHS):
            left = lefts[z]
            n_in, n_out = rows + 2 * left + 2 * HALF, rows + 2 * left
            source = held[z]
            for n in range(counts[z]):
                wide = 2 * LANE if (n + 2) * LANE <= source.shape[-1] else LANE
                window = source[:, :, n * LANE : n * LANE + wide].reshape(2 * n_in, wide)
                y = across(window, rec_op[f, starts[z] + n, :, :wide])
                at = slice(n * LANE, (n + 1) * LANE)
                q[0, :n_in, at] = (y[:n_in, :LANE] - y[n_in:, LANE:]).astype(BF)
                q[1, :n_in, at] = (y[:n_in, LANE:] + y[n_in:, :LANE]).astype(BF)
            op = (src_op0, src_op1, src_op2)[z][f, :, :n_in]
            reals = []
            for n in range(counts[z]):
                at = slice(n * LANE, (n + 1) * LANE)
                pair = jnp.concatenate([q[0, :n_in, at], q[1, :n_in, at]], axis=1)
                y = jnp.dot(op, pair, preferred_element_type=F32)
                real = (y[:n_out, :LANE] - y[n_out:, LANE:]).astype(BF)
                imag = (y[:n_out, LANE:] + y[n_out:, :LANE]).astype(BF)
                if z + 1 < DEPTHS:
                    held[z + 1][0, :, at] = real
                    held[z + 1][1, :, at] = imag
                else:
                    fin[0, f, :, at] = real
                    fin[1, f, :, at] = imag
                reals.append(real[left : left + rows, :].astype(F32))
            whole = jnp.concatenate(reals, axis=1) if left else None
            if left:
                whole = pltpu.roll(whole, whole.shape[1] - left, 1)
            for t in range(tiles):
                at = slice(t * LANE, (t + 1) * LANE)
                term = weights[z, :, at] * (whole[:, at] if left else reals[t])
                if z == 0 and f == 0:
                    part[:, at] = term
                elif z + 1 == DEPTHS and f == n_f - 1:
                    part_bf[:, at] = (part[:, at] + term).astype(BF)
                else:
                    part[:, at] = part[:, at] + term

    for d in range(1, n_freq):

        @pl.when(rank + d < n_freq)
        def _(d=d):
            pl.semaphore_wait(peer_ready.at[d - 1], 1)

    piece = rows // n_freq
    for d in range(1, n_freq):
        to = lax.rem(g + d, n_freq)
        copy = pltpu.make_async_remote_copy(
            src_ref=part_bf.at[pl.ds(pl.multiple_of(to * piece, piece), piece)],
            dst_ref=parts_in.at[d - 1],
            send_sem=part_send.at[d - 1],
            recv_sem=part_recv.at[d - 1],
            device_id={"freq": to},
            device_id_type=MESH,
        )
        copy.start()
        sends.append(copy)
    part_own[...] = part_bf[pl.ds(pl.multiple_of(g * piece, piece), piece), :]
    for f in range(n_f):
        for number, way in enumerate(ways):

            @pl.when(exists(way))
            def _(f=f, number=number, way=way):
                if f == 0 and number < 4:
                    index_copy(number, way).wait_send()
                halo_copy(f, number, way).wait_send()

    for copy in sends:
        copy.wait()


def finish(scale, fin, part_own, parts_in, wave_out, image_out, image, sems):
    copies = [
        pltpu.make_async_copy(fin, wave_out, sems.at[0]),
        pltpu.make_async_copy(image, image_out, sems.at[1]),
    ]
    copies[0].start()
    total = part_own[...].astype(F32)
    for d in range(parts_in.shape[0]):
        total = total + parts_in[d].astype(F32)
    image[...] = total * scale
    copies[1].start()
    for copy in copies:
        copy.wait()


def shards(wave, tap_table, src_index, rec_index, offset_bin, bin_weight):
    n_src, n_rec, n_freq = (lax.axis_size(a) for a in ("src", "rec", "freq"))
    _, n_f, rows, cols = wave.shape
    scale = 1.0 / math.sqrt(n_f * n_freq * DEPTHS)
    tiles = cols // LANE
    piece = rows // n_freq
    outs = [rows + 2 * (HALO - HALF * (z + 1)) for z in range(DEPTHS)]
    vmem = pl.BlockSpec(memory_space=pltpu.VMEM)
    hbm = pl.BlockSpec(memory_space=pltpu.HBM)
    dma = pltpu.SemaphoreType.DMA
    operands = [
        pltpu.with_memory_space_constraint(x, pltpu.HBM)
        for x in (wave, jnp.transpose(tap_table, (0, 3, 2, 1)), src_index, rec_index, offset_bin, bin_weight)
    ]
    results = pl.pallas_call(
        functools.partial(kernel, (n_src, n_rec, n_freq)),
        out_shape=(
            pltpu.VMEM(wave.shape, BF),
            pltpu.VMEM((piece, cols), BF),
            pltpu.VMEM((n_freq - 1, piece, cols), BF),
        ),
        in_specs=[hbm] * 6,
        out_specs=(vmem, vmem, vmem),
        scratch_shapes=[
            pltpu.VMEM((2, TAPS, n_f, tap_table.shape[1]), F32),
            pltpu.VMEM(src_index.shape, jnp.int32),
            pltpu.VMEM(rec_index.shape, jnp.int32),
            pltpu.VMEM(offset_bin.shape, jnp.int32),
            pltpu.VMEM(bin_weight.shape, F32),
            dma((5,)),
            pltpu.VMEM((n_f, 2, rows + 2 * HALO, cols + 2 * PAD), BF),
            pltpu.VMEM((2, outs[0], cols + LANE), BF),
            pltpu.VMEM((2, outs[1], cols + LANE), BF),
            pltpu.VMEM((2, rows + 2 * HALO, cols + LANE), BF),
            pltpu.VMEM((DEPTHS, rows), jnp.int32),
            pltpu.VMEM((DEPTHS, rows), jnp.int32),
            pltpu.VMEM((DEPTHS, PAD), jnp.int32),
            pltpu.VMEM((DEPTHS, PAD), jnp.int32),
            pltpu.VMEM((3 * rows, DEPTHS), F32),
            pltpu.VMEM((cols + 2 * PAD, DEPTHS), F32),
            pltpu.VMEM((n_f * 2 * LANE, tap_table.shape[1]), BF),
            pltpu.VMEM((3 * tiles + 2, LANE, n_f * 2 * LANE), F32),
            pltpu.VMEM((n_f, 3 * tiles + 2, 2 * LANE, 2 * LANE), BF),
            pltpu.VMEM((n_f, 2 * outs[0], 2 * LANE), BF),
            pltpu.VMEM((n_f, 2 * outs[1], LANE), BF),
            pltpu.VMEM((n_f, 2 * outs[2], LANE), BF),
            pltpu.VMEM((DEPTHS, rows, cols), F32),
            pltpu.VMEM((rows, cols), F32),
            pltpu.VMEM((rows, cols), BF),
            dma((n_f,)),
            dma((n_f, 8)),
            dma((n_f, 8)),
            dma((4,)),
            dma((4,)),
            dma((n_freq - 1,)),
            dma((n_freq - 1,)),
            pltpu.SemaphoreType.REGULAR((8,)),
            pltpu.SemaphoreType.REGULAR((n_freq - 1,)),
        ],
        compiler_params=pltpu.CompilerParams(
            collective_id=0, has_side_effects=True, vmem_limit_bytes=40 * 1024 * 1024
        ),
    )(*operands)
    return pl.pallas_call(
        functools.partial(finish, scale),
        out_shape=(
            jax.ShapeDtypeStruct(wave.shape, BF),
            jax.ShapeDtypeStruct((piece, cols), F32),
        ),
        in_specs=[vmem] * 3,
        out_specs=(hbm, hbm),
        scratch_shapes=[pltpu.VMEM((piece, cols), F32), dma((2,))],
        compiler_params=pltpu.CompilerParams(vmem_limit_bytes=4 * 1024 * 1024),
    )(*[pltpu.with_memory_space_constraint(x, pltpu.VMEM) for x in results])


def solution(mesh):
    placed = (
        P(None, "freq", "src", "rec"),
        P(None, None, "freq", None),
        P(None, "src"),
        P(None, "rec"),
        P("src", "rec"),
        P(),
    )
    return jax.shard_map(
        shards,
        mesh=mesh,
        in_specs=placed,
        out_specs=(P(None, "freq", "src", "rec"), P(("src", "freq"), "rec")),
        check_vma=False,
    )
```

```python
import functools
import math

import jax
import jax.numpy as jnp
from jax import lax
from jax.experimental import pallas as pl
from jax.experimental.pallas import tpu as pltpu
from jax.sharding import PartitionSpec as P

MESH = pl.DeviceIdType.MESH
TAPS = 33
HALF = TAPS // 2
DEPTHS = 3
HALO = HALF * DEPTHS
LANE = 128
PAD = LANE
BF = jnp.bfloat16
F32 = jnp.float32


def across(a, b):
    return lax.dot_general(a, b, (((1,), (1,)), ((), ())), preferred_element_type=F32)


def columns_of(rows):
    n = rows.shape[1]
    eye = lax.broadcasted_iota(jnp.int32, (n, n), 0) == lax.broadcasted_iota(jnp.int32, (n, n), 1)
    return across(eye.astype(BF), rows.astype(F32).astype(BF))


def onehot_of(column, entries):
    places = lax.broadcasted_iota(jnp.int32, (column.shape[0], entries), 1).astype(F32)
    return jnp.where(column == places, 1.0, 0.0).astype(BF)


def band(taps, base):
    m = taps.shape[0]
    turned = pltpu.roll(taps, base, 1, stride=1, stride_axis=0)
    lane = lax.broadcasted_iota(jnp.int32, (m, LANE), 1)
    row = lax.broadcasted_iota(jnp.int32, (m, LANE), 0)
    place = lane - row - base
    first = jnp.where(place >= 0, turned, 0.0)
    second = jnp.where((place < 0) & (place >= -LANE), turned, 0.0)
    return first.astype(BF), second.astype(BF)


def kernel(
    sizes,
    wave,
    table_in,
    src_index_in,
    rec_index_in,
    offset_bin_in,
    bin_weight_in,
    fin,
    part_own,
    parts_in,
    table,
    src_index,
    rec_index,
    offset_bin,
    bin_weight,
    in_sem,
    x0,
    x1,
    x2,
    q,
    src_low,
    src_high,
    rec_low,
    rec_high,
    src_col,
    rec_col,
    taps_table,
    rec_taps,
    rec_op,
    src_op0,
    src_op1,
    src_op2,
    weights,
    part,
    part_bf,
    own_sem,
    send_sem,
    recv_sem,
    index_send,
    index_recv,
    part_send,
    part_recv,
    ready,
    peer_ready,
    edges,
    corners,
):
    n_src, n_rec, n_freq = sizes
    _, n_f, rows, cols = wave.shape
    entries = table.shape[3]
    tiles = cols // LANE
    i, j, g = lax.axis_index("src"), lax.axis_index("rec"), lax.axis_index("freq")
    has = {-1: (i > 0, j > 0), 0: (None, None), 1: (i < n_src - 1, j < n_rec - 1)}
    ways = [(-1, 0), (1, 0), (0, -1), (0, 1), (-1, -1), (-1, 1), (1, -1), (1, 1)]

    def exists(way):
        conds = [c for c in (has[way[0]][0], has[way[1]][1]) if c is not None]
        return functools.reduce(jnp.logical_and, conds)

    def target(way):
        where = {}
        if way[0]:
            where["src"] = i + way[0]
        if way[1]:
            where["rec"] = j + way[1]
        return where

    is_origin = (i == 0) & (j == 0) & (g == 0)
    rank = jnp.where((i == 0) & (j == 0), lax.rem(g + n_freq - 1, n_freq), g)

    def toward_first(way):
        return (i + way[0] == 0) & (j + way[1] == 0) & (g == 0)

    def greets(way):
        side = exists(way) & jnp.logical_not(is_origin)
        return side & toward_first(way) if way[1] < 0 else side

    def greeted(way):
        side = exists(way) & jnp.logical_not(toward_first(way))
        return side & is_origin if way[1] > 0 else side

    barrier = pltpu.get_barrier_semaphore()
    for way in ways:

        @pl.when(greets(way))
        def _(way=way):
            pl.semaphore_signal(barrier, inc=1, device_id=target(way), device_id_type=MESH)

    for d in range(1, n_freq):

        @pl.when(rank + d < n_freq)
        def _(d=d):
            pl.semaphore_signal(
                barrier, inc=1, device_id={"freq": lax.rem(g + d, n_freq)}, device_id_type=MESH
            )

    def open_up():
        pl.semaphore_wait(barrier, sum(greeted(way).astype(jnp.int32) for way in ways) + rank)
        for number, way in enumerate(ways):

            @pl.when(greeted(way) & jnp.logical_not(greets(way)))
            def _(number=number, way=way):
                pl.semaphore_signal(
                    ready.at[number], inc=1, device_id=target(way), device_id_type=MESH
                )

        for d in range(1, n_freq):

            @pl.when(rank >= d)
            def _(d=d):
                pl.semaphore_signal(
                    peer_ready.at[d - 1],
                    inc=1,
                    device_id={"freq": lax.rem(g + n_freq - d, n_freq)},
                    device_id_type=MESH,
                )

    pl.when(is_origin)(open_up)

    fetch = [
        pltpu.make_async_copy(source, dest, in_sem.at[k])
        for k, (source, dest) in enumerate(
            [
                (src_index_in, src_index),
                (rec_index_in, rec_index),
                (table_in, table),
                (bin_weight_in, bin_weight),
                (offset_bin_in, offset_bin),
            ]
        )
    ]
    for copy in fetch:
        copy.start()
    own = [
        pltpu.make_async_copy(
            wave.at[:, f],
            x0.at[f, :, pl.ds(HALO, rows), pl.ds(PAD, cols)],
            own_sem.at[f],
        )
        for f in range(n_f)
    ]
    for copy in own:
        copy.start()

    def halo_copy(f, number, way):
        ds, dr = way
        from_rows = [pl.ds(HALO, rows), pl.ds(rows, HALO), pl.ds(HALO, HALO)][ds]
        to_rows = [pl.ds(HALO, rows), pl.ds(0, HALO), pl.ds(HALO + rows, HALO)][ds]
        from_cols = [pl.ds(PAD, cols), pl.ds(cols, PAD), pl.ds(PAD, PAD)][dr]
        to_cols = [pl.ds(PAD, cols), pl.ds(0, PAD), pl.ds(PAD + cols, PAD)][dr]
        source, dest = x0.at[f, :, from_rows, from_cols], x0.at[f, :, to_rows, to_cols]
        if ds and dr:
            source = edges.at[f, int(dr > 0), pl.ds(0 if ds < 0 else rows - HALO, HALO)]
            dest = corners.at[f, number - 4]
        return pltpu.make_async_remote_copy(
            src_ref=source,
            dst_ref=dest,
            send_sem=send_sem.at[f, number],
            recv_sem=recv_sem.at[f, number],
            device_id=target(way),
            device_id_type=MESH,
        )

    def index_copy(number, way):
        if way[0]:
            source, dest = src_index_in, (src_high if way[0] < 0 else src_low)
        elif way[1] < 0:
            source, dest = rec_index_in.at[:, pl.ds(0, PAD)], rec_high
        else:
            source, dest = rec_index_in.at[:, pl.ds(cols - PAD, PAD)], rec_low
        return pltpu.make_async_remote_copy(
            src_ref=source,
            dst_ref=dest,
            send_sem=index_send.at[number],
            recv_sem=index_recv.at[number],
            device_id=target(way),
            device_id_type=MESH,
        )

    counts = [tiles + 1, tiles + 1, tiles]
    starts = [0, counts[0], counts[0] + counts[1]]
    lefts = [HALO - HALF * (z + 1) for z in range(DEPTHS)]

    def build_rec(z, blocks):
        base = PAD - lefts[z] - HALF if z == 0 else 0
        for n in blocks:
            at = n * LANE + PAD - lefts[z]
            hot = onehot_of(rec_col[at : at + LANE, z : z + 1], entries)
            slot = starts[z] + n
            rec_taps[slot] = across(hot, taps_table[...])
        for n in blocks:
            slot = starts[z] + n
            for f in range(n_f):
                for c in range(2):
                    first = (2 * f + c) * LANE
                    low, high = band(rec_taps[slot, :, first : first + LANE], base)
                    rec_op[f, slot, c * LANE : (c + 1) * LANE, :LANE] = low
                    rec_op[f, slot, c * LANE : (c + 1) * LANE, LANE:] = high

    def build_src(z):
        op = (src_op0, src_op1, src_op2)[z]
        n_out = rows + 2 * lefts[z]
        hot = onehot_of(src_col[rows - lefts[z] : rows - lefts[z] + n_out, z : z + 1], entries)
        taps = across(hot, taps_table[...])
        for f in range(n_f):
            for c in range(2):
                low, high = band(taps[:, (2 * f + c) * LANE : (2 * f + c + 1) * LANE], 0)
                op[f, c * n_out : (c + 1) * n_out, :LANE] = low
                if op.shape[2] > LANE:
                    op[f, c * n_out : (c + 1) * n_out, LANE:] = high

    half = LANE // 2
    low_half = lax.broadcasted_iota(jnp.int32, (rows, LANE), 1) < half
    for f in range(n_f):
        own[f].wait()
        for side, at in enumerate((PAD, cols)):
            real, imag = (
                x0[f, c, HALO : HALO + rows, at : at + LANE].astype(F32) for c in range(2)
            )
            keep = low_half if side == 0 else jnp.logical_not(low_half)
            edges[f, side] = jnp.where(keep, real, pltpu.roll(imag, half, 1)).astype(BF)
    pl.when(jnp.logical_not(is_origin))(open_up)

    def send(f, number, way):
        if f == 0 and number < 4:
            index_copy(number, way).start()
        halo_copy(f, number, way).start()

    for group in ((4, 6, 2), (0, 1, 3, 5, 7)):
        for f in range(n_f):
            for number in group:

                @pl.when(greeted(ways[number]))
                def _(f=f, number=number):
                    send(f, number, ways[number])

    for way in ways:

        @pl.when(jnp.logical_not(exists(way)))
        def _(way=way):
            ds, dr = way
            at_rows = [slice(HALO, HALO + rows), slice(HALO + rows, None), slice(0, HALO)][ds]
            at_cols = [slice(PAD, PAD + cols), slice(PAD + cols, None), slice(0, PAD)][dr]
            for f in range(n_f):
                for c in range(2):
                    shape = x0[f, c, at_rows, at_cols].shape
                    x0[f, c, at_rows, at_cols] = jnp.zeros(shape, BF)
            if ds == 0 or dr == 0:
                ref = ((rec_high, rec_low) if ds == 0 else (src_high, src_low))[ds + dr < 0]
                ref[...] = jnp.full(ref.shape, -1, jnp.int32)

    taps_table[...] = jnp.zeros(taps_table.shape, BF)
    for copy in fetch:
        copy.wait()
    for f in range(n_f):
        for c in range(2):
            first = (2 * f + c) * LANE
            taps_table[first : first + TAPS, :] = table[c, :, f, :].astype(BF)

    src_col[rows : 2 * rows, :] = columns_of(src_index[...])
    for t in range(tiles):
        rec_col[PAD + t * LANE : PAD + (t + 1) * LANE, :] = columns_of(
            rec_index[:, t * LANE : (t + 1) * LANE]
        )
    for z in range(DEPTHS):
        build_rec(z, range(counts[z]) if lefts[z] == 0 else range(1, counts[z] - 1))
        if lefts[z] == 0:
            build_src(z)

    for t in range(tiles):
        at = slice(t * LANE, (t + 1) * LANE)
        bins = offset_bin[:, at]
        for z in range(DEPTHS):
            line = jnp.concatenate(
                [bin_weight[z : z + 1, :], jnp.zeros((1, LANE - bin_weight.shape[1]), F32)], axis=1
            )
            spread = jnp.broadcast_to(line, (rows, LANE))
            weights[z, :, at] = jnp.take_along_axis(
                spread, bins, axis=1, mode="promise_in_bounds"
            )

    for down in (False, True):
        for number, way in enumerate(ways):
            if (way[1] > 0) != down and (not down or max(way) <= 0):

                @pl.when(greets(way) & jnp.logical_not(greeted(way)))
                def _(number=number, way=way):
                    back = ways.index((-way[0], -way[1]))
                    pl.semaphore_wait(ready.at[back], 1)
                    for f in range(n_f):
                        send(f, number, way)

    for number, way in enumerate(ways[:4]):

        @pl.when(exists((-way[0], -way[1])))
        def _(number=number, way=way):
            index_copy(number, way).wait_recv()

    src_col[:rows, :] = columns_of(src_low[...])
    src_col[2 * rows :, :] = columns_of(src_high[...])
    rec_col[:PAD, :] = columns_of(rec_low[...])
    rec_col[PAD + cols :, :] = columns_of(rec_high[...])
    for z in range(DEPTHS):
        if lefts[z]:
            build_rec(z, (0, counts[z] - 1))
            build_src(z)

    sends = []
    for f in range(n_f):
        for number, way in enumerate(ways):

            @pl.when(exists((-way[0], -way[1])))
            def _(f=f, number=number, way=way):
                halo_copy(f, number, way).wait_recv()
                if way[0] and way[1]:
                    at_rows = [None, slice(0, HALO), slice(HALO + rows, None)][way[0]]
                    at_cols = [None, slice(0, PAD), slice(PAD + cols, None)][way[1]]
                    pair = corners[f, number - 4]
                    x0[f, 0, at_rows, at_cols] = pair
                    x0[f, 1, at_rows, at_cols] = pltpu.roll(pair.astype(F32), half, 1).astype(BF)

        held = (x0.at[f], x1, x2)
        for z in range(DEPTHS):
            left = lefts[z]
            n_in, n_out = rows + 2 * left + 2 * HALF, rows + 2 * left
            source = held[z]
            for n in range(counts[z]):
                wide = 2 * LANE if (n + 2) * LANE <= source.shape[-1] else LANE
                window = source[:, :, n * LANE : n * LANE + wide].reshape(2 * n_in, wide)
                y = across(window, rec_op[f, starts[z] + n, :, :wide])
                at = slice(n * LANE, (n + 1) * LANE)
                q[0, :n_in, at] = (y[:n_in, :LANE] - y[n_in:, LANE:]).astype(BF)
                q[1, :n_in, at] = (y[:n_in, LANE:] + y[n_in:, :LANE]).astype(BF)
            op = (src_op0, src_op1, src_op2)[z][f, :, :n_in]
            reals = []
            for n in range(counts[z]):
                at = slice(n * LANE, (n + 1) * LANE)
                pair = jnp.concatenate([q[0, :n_in, at], q[1, :n_in, at]], axis=1)
                y = jnp.dot(op, pair, preferred_element_type=F32)
                real = (y[:n_out, :LANE] - y[n_out:, LANE:]).astype(BF)
                imag = (y[:n_out, LANE:] + y[n_out:, :LANE]).astype(BF)
                if z + 1 < DEPTHS:
                    held[z + 1][0, :, at] = real
                    held[z + 1][1, :, at] = imag
                else:
                    fin[0, f, :, at] = real
                    fin[1, f, :, at] = imag
                reals.append(real[left : left + rows, :].astype(F32))
            whole = jnp.concatenate(reals, axis=1) if left else None
            if left:
                whole = pltpu.roll(whole, whole.shape[1] - left, 1)
            for t in range(tiles):
                at = slice(t * LANE, (t + 1) * LANE)
                term = weights[z, :, at] * (whole[:, at] if left else reals[t])
                if z == 0 and f == 0:
                    part[:, at] = term
                elif z + 1 == DEPTHS and f == n_f - 1:
                    part_bf[:, at] = (part[:, at] + term).astype(BF)
                else:
                    part[:, at] = part[:, at] + term

    for d in range(1, n_freq):

        @pl.when(rank + d < n_freq)
        def _(d=d):
            pl.semaphore_wait(peer_ready.at[d - 1], 1)

    piece = rows // n_freq
    for d in range(1, n_freq):
        to = lax.rem(g + d, n_freq)
        copy = pltpu.make_async_remote_copy(
            src_ref=part_bf.at[pl.ds(pl.multiple_of(to * piece, piece), piece)],
            dst_ref=parts_in.at[d - 1],
            send_sem=part_send.at[d - 1],
            recv_sem=part_recv.at[d - 1],
            device_id={"freq": to},
            device_id_type=MESH,
        )
        copy.start()
        sends.append(copy)
    part_own[...] = part_bf[pl.ds(pl.multiple_of(g * piece, piece), piece), :]
    for f in range(n_f):
        for number, way in enumerate(ways):

            @pl.when(exists(way))
            def _(f=f, number=number, way=way):
                if f == 0 and number < 4:
                    index_copy(number, way).wait_send()
                halo_copy(f, number, way).wait_send()

    for copy in sends:
        copy.wait()


def finish(scale, fin, part_own, parts_in, wave_out, image_out, image, sems):
    copies = [
        pltpu.make_async_copy(fin, wave_out, sems.at[0]),
        pltpu.make_async_copy(image, image_out, sems.at[1]),
    ]
    copies[0].start()
    total = part_own[...].astype(F32)
    for d in range(parts_in.shape[0]):
        total = total + parts_in[d].astype(F32)
    image[...] = total * scale
    copies[1].start()
    for copy in copies:
        copy.wait()


def shards(wave, tap_table, src_index, rec_index, offset_bin, bin_weight):
    n_src, n_rec, n_freq = (lax.axis_size(a) for a in ("src", "rec", "freq"))
    _, n_f, rows, cols = wave.shape
    scale = 1.0 / math.sqrt(n_f * n_freq * DEPTHS)
    tiles = cols // LANE
    piece = rows // n_freq
    outs = [rows + 2 * (HALO - HALF * (z + 1)) for z in range(DEPTHS)]
    vmem = pl.BlockSpec(memory_space=pltpu.VMEM)
    hbm = pl.BlockSpec(memory_space=pltpu.HBM)
    dma = pltpu.SemaphoreType.DMA
    operands = [
        pltpu.with_memory_space_constraint(x, pltpu.HBM)
        for x in (wave, jnp.transpose(tap_table, (0, 3, 2, 1)), src_index, rec_index, offset_bin, bin_weight)
    ]
    results = pl.pallas_call(
        functools.partial(kernel, (n_src, n_rec, n_freq)),
        out_shape=(
            pltpu.VMEM(wave.shape, BF),
            pltpu.VMEM((piece, cols), BF),
            pltpu.VMEM((n_freq - 1, piece, cols), BF),
        ),
        in_specs=[hbm] * 6,
        out_specs=(vmem, vmem, vmem),
        scratch_shapes=[
            pltpu.VMEM((2, TAPS, n_f, tap_table.shape[1]), F32),
            pltpu.VMEM(src_index.shape, jnp.int32),
            pltpu.VMEM(rec_index.shape, jnp.int32),
            pltpu.VMEM(offset_bin.shape, jnp.int32),
            pltpu.VMEM(bin_weight.shape, F32),
            dma((5,)),
            pltpu.VMEM((n_f, 2, rows + 2 * HALO, cols + 2 * PAD), BF),
            pltpu.VMEM((2, outs[0], cols + LANE), BF),
            pltpu.VMEM((2, outs[1], cols + LANE), BF),
            pltpu.VMEM((2, rows + 2 * HALO, cols + LANE), BF),
            pltpu.VMEM((DEPTHS, rows), jnp.int32),
            pltpu.VMEM((DEPTHS, rows), jnp.int32),
            pltpu.VMEM((DEPTHS, PAD), jnp.int32),
            pltpu.VMEM((DEPTHS, PAD), jnp.int32),
            pltpu.VMEM((3 * rows, DEPTHS), F32),
            pltpu.VMEM((cols + 2 * PAD, DEPTHS), F32),
            pltpu.VMEM((n_f * 2 * LANE, tap_table.shape[1]), BF),
            pltpu.VMEM((3 * tiles + 2, LANE, n_f * 2 * LANE), F32),
            pltpu.VMEM((n_f, 3 * tiles + 2, 2 * LANE, 2 * LANE), BF),
            pltpu.VMEM((n_f, 2 * outs[0], 2 * LANE), BF),
            pltpu.VMEM((n_f, 2 * outs[1], LANE), BF),
            pltpu.VMEM((n_f, 2 * outs[2], LANE), BF),
            pltpu.VMEM((DEPTHS, rows, cols), F32),
            pltpu.VMEM((rows, cols), F32),
            pltpu.VMEM((rows, cols), BF),
            dma((n_f,)),
            dma((n_f, 8)),
            dma((n_f, 8)),
            dma((4,)),
            dma((4,)),
            dma((n_freq - 1,)),
            dma((n_freq - 1,)),
            pltpu.SemaphoreType.REGULAR((8,)),
            pltpu.SemaphoreType.REGULAR((n_freq - 1,)),
            pltpu.VMEM((n_f, 2, rows, LANE), BF),
            pltpu.VMEM((n_f, 4, HALO, LANE), BF),
        ],
        compiler_params=pltpu.CompilerParams(
            collective_id=0, has_side_effects=True, vmem_limit_bytes=40 * 1024 * 1024
        ),
    )(*operands)
    return pl.pallas_call(
        functools.partial(finish, scale),
        out_shape=(
            jax.ShapeDtypeStruct(wave.shape, BF),
            jax.ShapeDtypeStruct((piece, cols), F32),
        ),
        in_specs=[vmem] * 3,
        out_specs=(hbm, hbm),
        scratch_shapes=[pltpu.VMEM((piece, cols), F32), dma((2,))],
        compiler_params=pltpu.CompilerParams(vmem_limit_bytes=4 * 1024 * 1024),
    )(*[pltpu.with_memory_space_constraint(x, pltpu.VMEM) for x in results])


def solution(mesh):
    placed = (
        P(None, "freq", "src", "rec"),
        P(None, None, "freq", None),
        P(None, "src"),
        P(None, "rec"),
        P("src", "rec"),
        P(),
    )
    return jax.shard_map(
        shards,
        mesh=mesh,
        in_specs=placed,
        out_specs=(P(None, "freq", "src", "rec"), P(("src", "freq"), "rec")),
        check_vma=False,
    )
```

```python
import functools
import math

import jax
import jax.numpy as jnp
from jax import lax
from jax.experimental import pallas as pl
from jax.experimental.pallas import tpu as pltpu
from jax.sharding import PartitionSpec as P

MESH = pl.DeviceIdType.MESH
TAPS = 33
HALF = TAPS // 2
DEPTHS = 3
HALO = HALF * DEPTHS
LANE = 128
PAD = LANE
BF = jnp.bfloat16
F32 = jnp.float32


def across(a, b):
    return lax.dot_general(a, b, (((1,), (1,)), ((), ())), preferred_element_type=F32)


def columns_of(rows):
    n = rows.shape[1]
    eye = lax.broadcasted_iota(jnp.int32, (n, n), 0) == lax.broadcasted_iota(jnp.int32, (n, n), 1)
    return across(eye.astype(BF), rows.astype(F32).astype(BF))


def onehot_of(column, entries):
    places = lax.broadcasted_iota(jnp.int32, (column.shape[0], entries), 1).astype(F32)
    return jnp.where(column == places, 1.0, 0.0).astype(BF)


def band(taps, base):
    m = taps.shape[0]
    turned = pltpu.roll(taps, base, 1, stride=1, stride_axis=0)
    lane = lax.broadcasted_iota(jnp.int32, (m, LANE), 1)
    row = lax.broadcasted_iota(jnp.int32, (m, LANE), 0)
    place = lane - row - base
    first = jnp.where(place >= 0, turned, 0.0)
    second = jnp.where((place < 0) & (place >= -LANE), turned, 0.0)
    return first.astype(BF), second.astype(BF)


def kernel(
    sizes,
    wave,
    table_in,
    src_index_in,
    rec_index_in,
    offset_bin_in,
    bin_weight_in,
    fin,
    part_own,
    parts_in,
    table,
    src_index,
    rec_index,
    offset_bin,
    bin_weight,
    in_sem,
    x0,
    x1,
    x2,
    q,
    src_low,
    src_high,
    rec_low,
    rec_high,
    src_col,
    rec_col,
    taps_table,
    rec_taps,
    rec_op,
    src_op0,
    src_op1,
    src_op2,
    weights,
    part,
    part_bf,
    own_sem,
    send_sem,
    recv_sem,
    index_send,
    index_recv,
    part_send,
    part_recv,
    ready,
    peer_ready,
):
    n_src, n_rec, n_freq = sizes
    _, n_f, rows, cols = wave.shape
    entries = table.shape[3]
    tiles = cols // LANE
    i, j, g = lax.axis_index("src"), lax.axis_index("rec"), lax.axis_index("freq")
    has = {-1: (i > 0, j > 0), 0: (None, None), 1: (i < n_src - 1, j < n_rec - 1)}
    ways = [(-1, 0), (1, 0), (0, -1), (0, 1), (-1, -1), (-1, 1), (1, -1), (1, 1)]

    def exists(way):
        conds = [c for c in (has[way[0]][0], has[way[1]][1]) if c is not None]
        return functools.reduce(jnp.logical_and, conds)

    def target(way):
        where = {}
        if way[0]:
            where["src"] = i + way[0]
        if way[1]:
            where["rec"] = j + way[1]
        return where

    is_origin = (i == 0) & (j == 0) & (g == 0)
    rank = jnp.where((i == 0) & (j == 0), lax.rem(g + n_freq - 1, n_freq), g)

    def toward_first(way):
        return (i + way[0] == 0) & (j + way[1] == 0) & (g == 0)

    def greets(way):
        side = exists(way) & jnp.logical_not(is_origin)
        return side & toward_first(way) if way[1] < 0 else side

    def greeted(way):
        side = exists(way) & jnp.logical_not(toward_first(way))
        return side & is_origin if way[1] > 0 else side

    barrier = pltpu.get_barrier_semaphore()
    for way in ways:

        @pl.when(greets(way))
        def _(way=way):
            pl.semaphore_signal(barrier, inc=1, device_id=target(way), device_id_type=MESH)

    for d in range(1, n_freq):

        @pl.when(rank + d < n_freq)
        def _(d=d):
            pl.semaphore_signal(
                barrier, inc=1, device_id={"freq": lax.rem(g + d, n_freq)}, device_id_type=MESH
            )

    fetch = [
        pltpu.make_async_copy(source, dest, in_sem.at[k])
        for k, (source, dest) in enumerate(
            [
                (src_index_in, src_index),
                (rec_index_in, rec_index),
                (table_in, table),
                (bin_weight_in, bin_weight),
                (offset_bin_in, offset_bin),
            ]
        )
    ]
    for copy in fetch:
        copy.start()
    own = [
        pltpu.make_async_copy(
            wave.at[:, f],
            x0.at[f, :, pl.ds(HALO, rows), pl.ds(PAD, cols)],
            own_sem.at[f],
        )
        for f in range(n_f)
    ]
    for copy in own:
        copy.start()

    def halo_copy(f, number, way):
        ds, dr = way
        from_rows = [pl.ds(0, rows), pl.ds(rows - HALO, HALO), pl.ds(0, HALO)][ds]
        to_rows = [pl.ds(HALO, rows), pl.ds(0, HALO), pl.ds(HALO + rows, HALO)][ds]
        from_cols = [pl.ds(0, cols), pl.ds(cols - PAD, PAD), pl.ds(0, PAD)][dr]
        to_cols = [pl.ds(PAD, cols), pl.ds(0, PAD), pl.ds(PAD + cols, PAD)][dr]
        return pltpu.make_async_remote_copy(
            src_ref=wave.at[:, f, from_rows, from_cols],
            dst_ref=x0.at[f, :, to_rows, to_cols],
            send_sem=send_sem.at[f, number],
            recv_sem=recv_sem.at[f, number],
            device_id=target(way),
            device_id_type=MESH,
        )

    def index_copy(number, way):
        if way[0]:
            source, dest = src_index_in, (src_high if way[0] < 0 else src_low)
        elif way[1] < 0:
            source, dest = rec_index_in.at[:, pl.ds(0, PAD)], rec_high
        else:
            source, dest = rec_index_in.at[:, pl.ds(cols - PAD, PAD)], rec_low
        return pltpu.make_async_remote_copy(
            src_ref=source,
            dst_ref=dest,
            send_sem=index_send.at[number],
            recv_sem=index_recv.at[number],
            device_id=target(way),
            device_id_type=MESH,
        )

    counts = [tiles + 1, tiles + 1, tiles]
    starts = [0, counts[0], counts[0] + counts[1]]
    lefts = [HALO - HALF * (z + 1) for z in range(DEPTHS)]

    def build_rec(z, blocks):
        base = PAD - lefts[z] - HALF if z == 0 else 0
        for n in blocks:
            at = n * LANE + PAD - lefts[z]
            hot = onehot_of(rec_col[at : at + LANE, z : z + 1], entries)
            slot = starts[z] + n
            rec_taps[slot] = across(hot, taps_table[...])
        for n in blocks:
            slot = starts[z] + n
            for f in range(n_f):
                for c in range(2):
                    first = (2 * f + c) * LANE
                    low, high = band(rec_taps[slot, :, first : first + LANE], base)
                    rec_op[f, slot, c * LANE : (c + 1) * LANE, :LANE] = low
                    rec_op[f, slot, c * LANE : (c + 1) * LANE, LANE:] = high

    def build_src(z):
        op = (src_op0, src_op1, src_op2)[z]
        n_out = rows + 2 * lefts[z]
        hot = onehot_of(src_col[rows - lefts[z] : rows - lefts[z] + n_out, z : z + 1], entries)
        taps = across(hot, taps_table[...])
        for f in range(n_f):
            for c in range(2):
                low, high = band(taps[:, (2 * f + c) * LANE : (2 * f + c + 1) * LANE], 0)
                op[f, c * n_out : (c + 1) * n_out, :LANE] = low
                if op.shape[2] > LANE:
                    op[f, c * n_out : (c + 1) * n_out, LANE:] = high

    pl.semaphore_wait(barrier, sum(greeted(way).astype(jnp.int32) for way in ways) + rank)
    for number, way in enumerate(ways):

        @pl.when(greeted(way) & jnp.logical_not(greets(way)))
        def _(number=number, way=way):
            pl.semaphore_signal(
                ready.at[number], inc=1, device_id=target(way), device_id_type=MESH
            )

    for d in range(1, n_freq):

        @pl.when(rank >= d)
        def _(d=d):
            pl.semaphore_signal(
                peer_ready.at[d - 1],
                inc=1,
                device_id={"freq": lax.rem(g + n_freq - d, n_freq)},
                device_id_type=MESH,
            )

    def send(f, number, way):
        if f == 0 and number < 4:
            index_copy(number, way).start()
        halo_copy(f, number, way).start()

    for group in ((4, 6, 2), (0, 1, 3, 5, 7)):
        for f in range(n_f):
            for number in group:

                @pl.when(greeted(ways[number]))
                def _(f=f, number=number):
                    send(f, number, ways[number])

    for way in ways:

        @pl.when(jnp.logical_not(exists(way)))
        def _(way=way):
            ds, dr = way
            at_rows = [slice(HALO, HALO + rows), slice(HALO + rows, None), slice(0, HALO)][ds]
            at_cols = [slice(PAD, PAD + cols), slice(PAD + cols, None), slice(0, PAD)][dr]
            for f in range(n_f):
                for c in range(2):
                    shape = x0[f, c, at_rows, at_cols].shape
                    x0[f, c, at_rows, at_cols] = jnp.zeros(shape, BF)
            if ds == 0 or dr == 0:
                ref = ((rec_high, rec_low) if ds == 0 else (src_high, src_low))[ds + dr < 0]
                ref[...] = jnp.full(ref.shape, -1, jnp.int32)

    taps_table[...] = jnp.zeros(taps_table.shape, BF)
    for copy in fetch:
        copy.wait()
    for f in range(n_f):
        for c in range(2):
            first = (2 * f + c) * LANE
            taps_table[first : first + TAPS, :] = table[c, :, f, :].astype(BF)

    src_col[rows : 2 * rows, :] = columns_of(src_index[...])
    for t in range(tiles):
        rec_col[PAD + t * LANE : PAD + (t + 1) * LANE, :] = columns_of(
            rec_index[:, t * LANE : (t + 1) * LANE]
        )
    for z in range(DEPTHS):
        build_rec(z, range(counts[z]) if lefts[z] == 0 else range(1, counts[z] - 1))

    for t in range(tiles):
        at = slice(t * LANE, (t + 1) * LANE)
        bins = offset_bin[:, at]
        for z in range(DEPTHS):
            line = jnp.concatenate(
                [bin_weight[z : z + 1, :], jnp.zeros((1, LANE - bin_weight.shape[1]), F32)], axis=1
            )
            spread = jnp.broadcast_to(line, (rows, LANE))
            weights[z, :, at] = jnp.take_along_axis(
                spread, bins, axis=1, mode="promise_in_bounds"
            )

    for down in (False, True):
        for number, way in enumerate(ways):
            if (way[1] > 0) != down and (not down or max(way) <= 0):

                @pl.when(greets(way) & jnp.logical_not(greeted(way)))
                def _(number=number, way=way):
                    back = ways.index((-way[0], -way[1]))
                    pl.semaphore_wait(ready.at[back], 1)
                    for f in range(n_f):
                        send(f, number, way)

    for number, way in enumerate(ways[:4]):

        @pl.when(exists((-way[0], -way[1])))
        def _(number=number, way=way):
            index_copy(number, way).wait_recv()

    src_col[:rows, :] = columns_of(src_low[...])
    src_col[2 * rows :, :] = columns_of(src_high[...])
    rec_col[:PAD, :] = columns_of(rec_low[...])
    rec_col[PAD + cols :, :] = columns_of(rec_high[...])
    for z in range(DEPTHS):
        if lefts[z]:
            build_rec(z, (0, counts[z] - 1))
        build_src(z)

    sends = []
    for f in range(n_f):
        own[f].wait()
        for number, way in enumerate(ways):

            @pl.when(exists((-way[0], -way[1])))
            def _(f=f, number=number, way=way):
                halo_copy(f, number, way).wait_recv()

        held = (x0.at[f], x1, x2)
        for z in range(DEPTHS):
            left = lefts[z]
            n_in, n_out = rows + 2 * left + 2 * HALF, rows + 2 * left
            source = held[z]
            for n in range(counts[z]):
                wide = 2 * LANE if (n + 2) * LANE <= source.shape[-1] else LANE
                window = source[:, :, n * LANE : n * LANE + wide].reshape(2 * n_in, wide)
                y = across(window, rec_op[f, starts[z] + n, :, :wide])
                at = slice(n * LANE, (n + 1) * LANE)
                q[0, :n_in, at] = (y[:n_in, :LANE] - y[n_in:, LANE:]).astype(BF)
                q[1, :n_in, at] = (y[:n_in, LANE:] + y[n_in:, :LANE]).astype(BF)
            op = (src_op0, src_op1, src_op2)[z][f, :, :n_in]
            reals = []
            for n in range(counts[z]):
                at = slice(n * LANE, (n + 1) * LANE)
                pair = jnp.concatenate([q[0, :n_in, at], q[1, :n_in, at]], axis=1)
                y = jnp.dot(op, pair, preferred_element_type=F32)
                real = (y[:n_out, :LANE] - y[n_out:, LANE:]).astype(BF)
                imag = (y[:n_out, LANE:] + y[n_out:, :LANE]).astype(BF)
                if z + 1 < DEPTHS:
                    held[z + 1][0, :, at] = real
                    held[z + 1][1, :, at] = imag
                else:
                    fin[0, f, :, at] = real
                    fin[1, f, :, at] = imag
                reals.append(real[left : left + rows, :].astype(F32))
            whole = jnp.concatenate(reals, axis=1) if left else None
            if left:
                whole = pltpu.roll(whole, whole.shape[1] - left, 1)
            for t in range(tiles):
                at = slice(t * LANE, (t + 1) * LANE)
                term = weights[z, :, at] * (whole[:, at] if left else reals[t])
                if z == 0 and f == 0:
                    part[:, at] = term
                elif z + 1 == DEPTHS and f == n_f - 1:
                    part_bf[:, at] = (part[:, at] + term).astype(BF)
                else:
                    part[:, at] = part[:, at] + term

    for d in range(1, n_freq):

        @pl.when(rank + d < n_freq)
        def _(d=d):
            pl.semaphore_wait(peer_ready.at[d - 1], 1)

    piece = rows // n_freq
    for d in sorted(range(1, n_freq), key=lambda d: d != n_freq // 2):
        to = lax.rem(g + d, n_freq)
        copy = pltpu.make_async_remote_copy(
            src_ref=part_bf.at[pl.ds(pl.multiple_of(to * piece, piece), piece)],
            dst_ref=parts_in.at[d - 1],
            send_sem=part_send.at[d - 1],
            recv_sem=part_recv.at[d - 1],
            device_id={"freq": to},
            device_id_type=MESH,
        )
        copy.start()
        sends.append(copy)
    part_own[...] = part_bf[pl.ds(pl.multiple_of(g * piece, piece), piece), :]
    for f in range(n_f):
        for number, way in enumerate(ways):

            @pl.when(exists(way))
            def _(f=f, number=number, way=way):
                if f == 0 and number < 4:
                    index_copy(number, way).wait_send()
                halo_copy(f, number, way).wait_send()

    for copy in sends:
        copy.wait()


def finish(scale, fin, part_own, parts_in, wave_out, image_out, image, sems):
    copies = [
        pltpu.make_async_copy(fin, wave_out, sems.at[0]),
        pltpu.make_async_copy(image, image_out, sems.at[1]),
    ]
    copies[0].start()
    total = part_own[...].astype(F32)
    for d in range(parts_in.shape[0]):
        total = total + parts_in[d].astype(F32)
    image[...] = total * scale
    copies[1].start()
    for copy in copies:
        copy.wait()


def shards(wave, tap_table, src_index, rec_index, offset_bin, bin_weight):
    n_src, n_rec, n_freq = (lax.axis_size(a) for a in ("src", "rec", "freq"))
    _, n_f, rows, cols = wave.shape
    scale = 1.0 / math.sqrt(n_f * n_freq * DEPTHS)
    tiles = cols // LANE
    piece = rows // n_freq
    outs = [rows + 2 * (HALO - HALF * (z + 1)) for z in range(DEPTHS)]
    vmem = pl.BlockSpec(memory_space=pltpu.VMEM)
    hbm = pl.BlockSpec(memory_space=pltpu.HBM)
    dma = pltpu.SemaphoreType.DMA
    operands = [
        pltpu.with_memory_space_constraint(x, pltpu.HBM)
        for x in (wave, jnp.transpose(tap_table, (0, 3, 2, 1)), src_index, rec_index, offset_bin, bin_weight)
    ]
    results = pl.pallas_call(
        functools.partial(kernel, (n_src, n_rec, n_freq)),
        out_shape=(
            pltpu.VMEM(wave.shape, BF),
            pltpu.VMEM((piece, cols), BF),
            pltpu.VMEM((n_freq - 1, piece, cols), BF),
        ),
        in_specs=[hbm] * 6,
        out_specs=(vmem, vmem, vmem),
        scratch_shapes=[
            pltpu.VMEM((2, TAPS, n_f, tap_table.shape[1]), F32),
            pltpu.VMEM(src_index.shape, jnp.int32),
            pltpu.VMEM(rec_index.shape, jnp.int32),
            pltpu.VMEM(offset_bin.shape, jnp.int32),
            pltpu.VMEM(bin_weight.shape, F32),
            dma((5,)),
            pltpu.VMEM((n_f, 2, rows + 2 * HALO, cols + 2 * PAD), BF),
            pltpu.VMEM((2, outs[0], cols + LANE), BF),
            pltpu.VMEM((2, outs[1], cols + LANE), BF),
            pltpu.VMEM((2, rows + 2 * HALO, cols + LANE), BF),
            pltpu.VMEM((DEPTHS, rows), jnp.int32),
            pltpu.VMEM((DEPTHS, rows), jnp.int32),
            pltpu.VMEM((DEPTHS, PAD), jnp.int32),
            pltpu.VMEM((DEPTHS, PAD), jnp.int32),
            pltpu.VMEM((3 * rows, DEPTHS), F32),
            pltpu.VMEM((cols + 2 * PAD, DEPTHS), F32),
            pltpu.VMEM((n_f * 2 * LANE, tap_table.shape[1]), BF),
            pltpu.VMEM((3 * tiles + 2, LANE, n_f * 2 * LANE), F32),
            pltpu.VMEM((n_f, 3 * tiles + 2, 2 * LANE, 2 * LANE), BF),
            pltpu.VMEM((n_f, 2 * outs[0], 2 * LANE), BF),
            pltpu.VMEM((n_f, 2 * outs[1], LANE), BF),
            pltpu.VMEM((n_f, 2 * outs[2], LANE), BF),
            pltpu.VMEM((DEPTHS, rows, cols), F32),
            pltpu.VMEM((rows, cols), F32),
            pltpu.VMEM((rows, cols), BF),
            dma((n_f,)),
            dma((n_f, 8)),
            dma((n_f, 8)),
            dma((4,)),
            dma((4,)),
            dma((n_freq - 1,)),
            dma((n_freq - 1,)),
            pltpu.SemaphoreType.REGULAR((8,)),
            pltpu.SemaphoreType.REGULAR((n_freq - 1,)),
        ],
        compiler_params=pltpu.CompilerParams(
            collective_id=0, has_side_effects=True, vmem_limit_bytes=40 * 1024 * 1024
        ),
    )(*operands)
    return pl.pallas_call(
        functools.partial(finish, scale),
        out_shape=(
            jax.ShapeDtypeStruct(wave.shape, BF),
            jax.ShapeDtypeStruct((piece, cols), F32),
        ),
        in_specs=[vmem] * 3,
        out_specs=(hbm, hbm),
        scratch_shapes=[pltpu.VMEM((piece, cols), F32), dma((2,))],
        compiler_params=pltpu.CompilerParams(vmem_limit_bytes=4 * 1024 * 1024),
    )(*[pltpu.with_memory_space_constraint(x, pltpu.VMEM) for x in results])


def solution(mesh):
    placed = (
        P(None, "freq", "src", "rec"),
        P(None, None, "freq", None),
        P(None, "src"),
        P(None, "rec"),
        P("src", "rec"),
        P(),
    )
    return jax.shard_map(
        shards,
        mesh=mesh,
        in_specs=placed,
        out_specs=(P(None, "freq", "src", "rec"), P(("src", "freq"), "rec")),
        check_vma=False,
    )
```
